128 devices in a mesh: ctx: 32 (over y, x_lo, z), pb: 4 (over x_hi, core).
Axes of the slice: x: 4 (x_hi: 2, x_lo: 2; x = x_hi * 2 + x_lo), y: 4, z: 4, core: 2. Of those that a mesh axis runs over, the one named last changes fastest.
Arguments:
- queries: bfloat16 [512, 128, 576], P('pb'), may hold values from -69 to 69
- key_cache: bfloat16 [16384, 576], P('ctx'), may hold values from -12 to 12
- index_queries: bfloat16 [64, 512, 128], P(None, 'pb'), may hold values from -47 to 47
- index_keys: bfloat16 [16384, 128], P('ctx'), may hold values from -12 to 12
- head_weights: float32 [512, 64], P('pb'), may hold values from 0.02 to 0.3
- positions: int32 [512], P('pb'), may hold values from 4096 to 16383
- valid_lengths: int32 [512], P('pb'), may hold values from 3 to 16384
Outputs:
- kl_loss: float32 [512], P('pb')
- key_grad: float32 [16384, 128], P('ctx')
- query_grad: float32 [64, 512, 128], P('ctx', 'pb')
- weight_grad: float32 [512, 64], P('pb')
The draws below stay inside these ranges and needn't reach their ends.
All inputs are finite; a program needn't handle non-finite values.
Results may differ from the reference program's by a relative error of at most 0.0023.
Values sent between devices are 32-bit elements; how exact they have to be, the bound alone decides.
A program may use at most 192 MiB of HBM per device.

```python
import math
import jax
import jax.numpy as jnp
from jax import lax

HEADS = 128
LAT = 576
IHEADS = 64
IDIM = 128
QUERIES = 512
CONTEXT = 16384


def shared_positions(key):
    own_key = jax.random.fold_in(key, 900)
    drawn = jax.random.randint(own_key, (QUERIES,), CONTEXT // 4, CONTEXT, dtype=jnp.int32)
    return drawn.at[0].set(CONTEXT // 4).at[QUERIES - 1].set(CONTEXT - 1)


def paired_rows(key, row_count, col_count):
    base = jax.random.normal(key, (row_count // 2, 2, col_count), jnp.float32)
    base = jnp.clip(base, -5.0, 5.0)
    even_rows = base[:, 0]
    odd_rows = base[:, 1]
    return jnp.stack([even_rows, odd_rows], axis=1).reshape(row_count, col_count)


def shared_cache(key):
    return paired_rows(jax.random.fold_in(key, 910), CONTEXT, LAT)


def shared_index_keys(key):
    return paired_rows(jax.random.fold_in(key, 920), CONTEXT, IDIM)


def anchor_rows(key):
    placed = shared_positions(key)
    return placed - 1 + placed % 2


def draw_positions(key, part):
    placed = shared_positions(key)
    return placed


def draw_key_cache(key, part):
    cache = shared_cache(key)
    return cache.astype(jnp.bfloat16)


def draw_index_keys(key, part):
    ikeys = shared_index_keys(key)
    return ikeys.astype(jnp.bfloat16)


def draw_queries(key, part):
    anchor = anchor_rows(key)
    cache = shared_cache(key)
    key = jax.random.fold_in(key, 5)
    entries = jax.random.normal(key, (QUERIES, HEADS, LAT), jnp.float32)
    target_score = jax.random.uniform(jax.random.fold_in(key, 6), (HEADS,), jnp.float32, 120.0, 300.0)
    strength = target_score * 192.0 ** 0.5 / LAT
    chosen = jnp.arange(QUERIES) % 8 == 0
    aimed = cache[anchor]
    entries = jnp.where(chosen[:, None, None], 0.3 * entries + strength[None, :, None] * aimed[:, None, :], entries)
    bound = float(40000 // LAT)
    return jnp.clip(entries, -bound, bound).astype(jnp.bfloat16)


def draw_index_queries(key, part):
    anchor = anchor_rows(key)
    ikeys = shared_index_keys(key)
    key = jax.random.fold_in(key, 7)
    entries = jax.random.normal(key, (IHEADS, QUERIES, IDIM), jnp.float32)
    target_logit = jax.random.uniform(jax.random.fold_in(key, 8), (IHEADS,), jnp.float32, 100.0, 250.0)
    strength = target_logit / (IDIM ** 0.5 * IHEADS * 0.1)
    chosen = jnp.arange(QUERIES) % 8 == 0
    aimed = ikeys[anchor]
    entries = jnp.where(chosen[None, :, None], 0.3 * entries + strength[:, None, None] * aimed[None, :, :], entries)
    bound = float(40 + 64000 // (IDIM * IHEADS))
    return jnp.clip(entries, -bound, bound).astype(jnp.bfloat16)


def with_ends(values, stream_key, smallest, high):
    shape = values.shape
    spot = [jax.random.randint(jax.random.fold_in(stream_key, axis), (), 0, shape[axis]) for axis in range(len(shape))]
    values = values.at[tuple(spot)].set(smallest)
    longest = shape.index(max(shape))
    spot[longest] = (spot[longest] + 1) % shape[longest]
    return values.at[tuple(spot)].set(high)


def levels(key, extent, pieces, smallest, largest):
    level, own = 1.0, jax.random.fold_in(key, 6)
    for position, shards_of in pieces:
        heights = jnp.exp(jax.random.uniform(jax.random.fold_in(own, position), (shards_of,), jnp.float32, smallest / len(pieces), largest / len(pieces)))
        level = level * jnp.repeat(heights, extent[position] // shards_of).reshape([-1 if axis == position else 1 for axis in range(len(extent))])
    return level


def setup_inputs(seed: int = 0) -> dict:
    arg_keys = jax.random.split(jax.random.key(seed), 8)
    return {
        "queries": draw_queries(jax.random.fold_in(arg_keys[7], 71), 0),
        "key_cache": draw_key_cache(jax.random.fold_in(arg_keys[7], 71), 0),
        "index_queries": draw_index_queries(jax.random.fold_in(arg_keys[7], 71), 0),
        "index_keys": draw_index_keys(jax.random.fold_in(arg_keys[7], 71), 0),
        "head_weights": jnp.clip(jnp.exp(math.log(0.3) - 2.7080503 * jax.random.uniform(arg_keys[4], (QUERIES, IHEADS), jnp.float32) ** levels(arg_keys[4], (QUERIES, IHEADS), ((0, 4),), -0.2, 0.2)), 0.02, 0.3),
        "positions": draw_positions(jax.random.fold_in(arg_keys[7], 71), 0),
        "valid_lengths": with_ends(jax.random.randint(arg_keys[6], (QUERIES,), 3, CONTEXT + 1), jax.random.fold_in(arg_keys[6], 1), 3, CONTEXT).astype(jnp.int32),
    }


NEG = -1e30
main_scale = 192 ** -0.5


def reference(queries, key_cache, index_queries, index_keys, head_weights, positions, valid_lengths):
    block_rows = 8
    block_count = QUERIES // block_rows
    keys_wide = key_cache.astype(jnp.float32)
    ikeys_wide = index_keys.astype(jnp.float32)
    iscale = IDIM ** -0.5
    loss_scale = CONTEXT / QUERIES
    key_index = jnp.arange(CONTEXT, dtype=jnp.int32)

    def one_block(carry, inputs):
        query_block, iquery_block, weight_block, pos_block, len_block = inputs
        valid_mask = (key_index[None, :] <= pos_block[:, None]) & (key_index[None, :] > (pos_block - len_block)[:, None])
        target = jnp.zeros((block_rows, CONTEXT), jnp.float32)
        for group_id in range(HEADS // 16):
            scores = jnp.einsum('qhc,tc->qht', query_block[:, group_id * 16:(group_id + 1) * 16].astype(jnp.float32), keys_wide) * main_scale
            scores = jnp.where(valid_mask[:, None, :], scores, NEG)
            row_peak = jnp.max(scores, axis=2, keepdims=True)
            expo = jnp.where(valid_mask[:, None, :], jnp.exp(scores - row_peak), 0.0)
            target = target + jnp.sum(expo / jnp.sum(expo, axis=2, keepdims=True), axis=1)
        target = target / HEADS
        index_raw = jnp.einsum('jqd,td->jqt', iquery_block.astype(jnp.float32), ikeys_wide)
        active = jnp.maximum(index_raw, 0.0)
        logits = jnp.sum(weight_block.T[:, :, None] * active, axis=0) * iscale
        logits = jnp.where(valid_mask, logits, NEG)
        index_peak = jnp.max(logits, axis=1, keepdims=True)
        index_exp = jnp.where(valid_mask, jnp.exp(logits - index_peak), 0.0)
        index_total = jnp.sum(index_exp, axis=1, keepdims=True)
        log_index = logits - index_peak - jnp.log(index_total)
        positive = valid_mask & (target > 0)
        safe_target = jnp.where(target > 0, target, 1.0)
        loss_rows = jnp.sum(jnp.where(positive, target * (jnp.log(safe_target) - log_index), 0.0), axis=1)
        dlogit = jnp.where(valid_mask, loss_scale * (index_exp / index_total - target), 0.0)
        weight_rows = jnp.sum(dlogit[None] * active, axis=2).T * iscale
        coefficient = jnp.where(index_raw > 0, dlogit[None] * weight_block.T[:, :, None] * iscale, 0.0).astype(jnp.bfloat16)
        coef_wide = coefficient.astype(jnp.float32)
        query_rows = jnp.einsum('jqt,td->jqd', coef_wide, ikeys_wide)
        carry = carry + jnp.einsum('jqt,jqd->td', coef_wide, iquery_block.astype(jnp.float32))
        return carry, (loss_rows, weight_rows, query_rows)

    query_blocks = queries.reshape(block_count, block_rows, HEADS, LAT)
    iquery_blocks = index_queries.reshape(IHEADS, block_count, block_rows, IDIM).transpose(1, 0, 2, 3)
    weight_blocks = head_weights.reshape(block_count, block_rows, IHEADS)
    pos_blocks = positions.reshape(block_count, block_rows)
    len_blocks = valid_lengths.reshape(block_count, block_rows)
    key_grad, outputs = lax.scan(one_block, jnp.zeros((CONTEXT, IDIM), jnp.float32),
                                 (query_blocks, iquery_blocks, weight_blocks, pos_blocks, len_blocks))
    loss_rows, weight_rows, query_rows = outputs
    kl_loss = loss_rows.reshape(QUERIES)
    weight_grad = weight_rows.reshape(QUERIES, IHEADS)
    query_grad = query_rows.transpose(1, 0, 2, 3).reshape(IHEADS, QUERIES, IDIM)
    return kl_loss, key_grad, query_grad, weight_grad
```

```python
import functools
import math

import jax
import jax.numpy as jnp
from jax import lax
from jax.experimental import pallas as pl
from jax.experimental.pallas import tpu as pltpu
from jax.sharding import PartitionSpec as P

NEG = -1e30
LOG2E = math.log2(math.e)
MESH = pl.DeviceIdType.MESH
F32 = jnp.float32
BF16 = jnp.bfloat16
ZGROUP = 4
QBLOCK = 8


def nt_dot(lhs, rhs):
    return lax.dot_general(lhs, rhs, (((1,), (1,)), ((), ())), preferred_element_type=F32)


def nn_dot(lhs, rhs):
    return jnp.dot(lhs, rhs, preferred_element_type=F32)


def wait_bytes(ref, sem):
    pltpu.make_async_copy(ref, ref, sem).wait()


def kernel(
    n_ctx, n_pb, loss_scale,
    q_hbm, kt_ref, iq_ref, ik_ref, wt_ref, pos_ref, len_ref,
    kl_ref, key_ref, qg_ref, wg_ref,
    qb, ke, s_ref, p_ref, logit_ref, dl_ref, fac_ref, fact_hi, fact_lo, f_ref, tacc,
    ikt_all, ik_all, coef, coef2,
    key_send, key_gather, dl_gather,
    ist_send, ist_recv, st_send, st_recv, lse_send, lse_recv,
    kp_ref, kp_recv, ko_ref, t_send, t_recv, w_send, w_recv, qs_ref, q_recv,
    q_sem, send_sem, recv_sem, zk_sem, zd_sem,
):
    ctx = lax.axis_index("ctx")
    pb = lax.axis_index("pb")
    z = lax.rem(ctx, ZGROUP)
    grp = ctx // ZGROUP
    n_grp = n_ctx // ZGROUP
    heads = iq_ref.shape[0]
    pairs = heads // 2
    queries, lat, lanes = q_hbm.shape
    t_rows = ik_ref.shape[0]
    idim = ik_ref.shape[1]
    blocks = queries // QBLOCK
    iscale = idim ** -0.5
    mscale = 192 ** -0.5 * LOG2E

    def ctx_peer(r):
        return lax.rem(ctx + r, n_ctx)

    def pb_peer(r):
        return lax.rem(pb + r, n_pb)

    def z_peer(r):
        return grp * ZGROUP + lax.rem(z + r, ZGROUP)

    barrier = pltpu.get_barrier_semaphore()

    @pl.loop(1, n_ctx)
    def _(r):
        pl.semaphore_signal(barrier, inc=1, device_id=(ctx_peer(r), pb), device_id_type=MESH)

    @pl.loop(1, n_pb)
    def _(r):
        pl.semaphore_signal(barrier, inc=1, device_id=(ctx, pb_peer(r)), device_id_type=MESH)

    def q_copy(block, slot):
        return pltpu.make_async_copy(
            q_hbm.at[pl.ds(block * QBLOCK, QBLOCK)],
            qb.at[slot, :, pl.ds(lanes, lat), :],
            q_sem.at[slot],
        )

    q_copy(0, 0).start()
    q_copy(1, 1).start()

    t_index = ctx * t_rows + lax.broadcasted_iota(jnp.int32, (t_rows, lanes), 0)
    pos = pos_ref[...]
    visible = (t_index <= pos) & (t_index > pos - len_ref[...])
    bias = jnp.where(visible, 0.0, NEG)
    ke[:, 0:lanes] = bias.astype(BF16)
    ke[:, lanes:lanes + lat] = kt_ref[...].astype(F32).T.astype(BF16)
    depth = ke.shape[1]
    pad = depth - lanes - lat
    ke[:, lanes + lat:] = jnp.zeros((t_rows, pad), BF16)
    for slot in range(2):
        for i in range(QBLOCK):
            qb[slot, i, lanes + lat:, :] = jnp.zeros((pad, lanes), BF16)

    ik = ik_ref[...]
    key_send[...] = ik.astype(F32)

    logit_ref[...] = jnp.zeros_like(logit_ref)

    @pl.loop(0, pairs // 4)
    def _(step):
        total = logit_ref[...]
        for u in range(4):
            jp = step * 4 + u
            raw = nt_dot(ik, iq_ref[pl.ds(2 * jp, 2)].reshape(2 * lanes, idim))
            w = wt_ref[pl.ds(2 * jp, 2), :]
            total = total + jnp.maximum(raw[:, :lanes], 0.0) * w[0:1]
            total = total + jnp.maximum(raw[:, lanes:], 0.0) * w[1:2]
        logit_ref[...] = total

    logits = logit_ref[...] * (iscale * LOG2E) + bias
    logit_ref[...] = logits
    i_peak = jnp.max(logits, axis=0, keepdims=True)
    i_sum = jnp.sum(jnp.exp2(logits - i_peak), axis=0, keepdims=True)
    ist_send[...] = jnp.zeros_like(ist_send)
    ist_send[0:1, :] = i_peak
    ist_send[1:2, :] = i_sum

    pl.semaphore_wait(barrier, n_ctx - 1 + n_pb - 1)

    for r in range(1, ZGROUP):
        pltpu.make_async_remote_copy(
            key_send, key_gather.at[r - 1], send_sem.at[0], zk_sem.at[r - 1],
            device_id=(z_peer(r), pb), device_id_type=MESH,
        ).start()

    @pl.loop(1, n_ctx)
    def _(r):
        pltpu.make_async_remote_copy(
            ist_send, ist_recv.at[r - 1], send_sem.at[1], recv_sem.at[1],
            device_id=(ctx_peer(r), pb), device_id_type=MESH,
        ).start()

    @pl.loop(0, blocks)
    def _(block):
        slot = lax.rem(block, 2)
        q_copy(block, slot).wait()
        row = lax.broadcasted_iota(jnp.int32, (lanes, lanes), 0)
        for i in range(QBLOCK):
            qb[slot, i, 0:lanes, :] = jnp.where(row == block * QBLOCK + i, 1.0, 0.0).astype(BF16)
        for u in range(QBLOCK // 2):
            rhs = jnp.concatenate([qb[slot, 2 * u], qb[slot, 2 * u + 1]], axis=1)
            s_ref[u % 2] = nn_dot(ke[...], rhs)
            s = s_ref[u % 2]
            peak = jnp.max(s, axis=0, keepdims=True) * mscale
            expo = jnp.exp2(s * mscale - peak)
            total = jnp.sum(expo, axis=0, keepdims=True)
            p_ref[block, :, 2 * u * lanes:(2 * u + 2) * lanes] = expo.astype(BF16)
            for h in range(2):
                i = 2 * u + h
                owner = block * (QBLOCK // 4) + i // 4
                st_send[owner, pl.ds(i % 4, 1), :] = peak[:, h * lanes:(h + 1) * lanes]
                st_send[owner, pl.ds(4 + i % 4, 1), :] = total[:, h * lanes:(h + 1) * lanes]

        @pl.when(block + 2 < blocks)
        def _():
            q_copy(block + 2, slot).start()

    @pl.loop(1, n_ctx)
    def _(r):
        peer = ctx_peer(r)
        pltpu.make_async_remote_copy(
            st_send.at[peer], st_recv.at[r - 1], send_sem.at[2], recv_sem.at[2],
            device_id=(peer, pb), device_id_type=MESH,
        ).start()

    ik_all[0:t_rows, :] = ik
    ikt_all[:, 0:t_rows] = key_send[...].T.astype(BF16)
    for r in range(1, ZGROUP):
        wait_bytes(key_gather.at[r - 1], zk_sem.at[r - 1])
        got = key_gather[r - 1]
        ik_all[r * t_rows:(r + 1) * t_rows, :] = got.astype(BF16)
        ikt_all[:, r * t_rows:(r + 1) * t_rows] = got.T.astype(BF16)

    wait_bytes(ist_recv.at[pl.ds(0, n_ctx - 1)], recv_sem.at[1])
    ist_recv[n_ctx - 1] = ist_send[...]
    got = ist_recv[...]
    peaks, sums = got[:, 0:1, :], got[:, 1:2, :]
    top = jnp.max(peaks, axis=0)
    i_lse = top + jnp.log(jnp.sum(sums * jnp.exp2(peaks - top[None]), axis=0)) * LOG2E

    wait_bytes(st_recv.at[pl.ds(0, n_ctx - 1)], recv_sem.at[2])
    st_recv[n_ctx - 1] = st_send[ctx]
    got = st_recv[...]
    peaks, sums = got[:, 0:4, :], got[:, 4:8, :]
    top = jnp.max(peaks, axis=0)
    lse = top + jnp.log(jnp.sum(sums * jnp.exp2(peaks - top[None]), axis=0)) * LOG2E
    lse_send[...] = jnp.zeros_like(lse_send)
    lse_send[0:4, :] = lse

    @pl.loop(1, n_ctx)
    def _(r):
        pltpu.make_async_remote_copy(
            lse_send, lse_recv.at[ctx], send_sem.at[3], recv_sem.at[3],
            device_id=(ctx_peer(r), pb), device_id_type=MESH,
        ).start()

    tacc[...] = jnp.zeros_like(tacc)
    wait_bytes(lse_recv.at[pl.ds(0, n_ctx - 1)], recv_sem.at[3])
    lse_recv[ctx] = lse_send[...]
    for i in range(n_ctx):
        fac_ref[4 * i:4 * i + 4, :] = jnp.exp2(st_send[i, 0:4, :] - lse_recv[i, 0:4, :])
    fact = fac_ref[...].T * (1.0 / lanes)
    hi = fact.astype(BF16)
    fact_hi[...] = hi.astype(F32)
    fact_lo[...] = fact - hi.astype(F32)

    @pl.loop(0, blocks)
    def _(block):
        lane = lax.broadcasted_iota(jnp.int32, (lanes, lanes), 1)
        for i in range(QBLOCK):
            here = lane == block * QBLOCK + i
            f_ref[i * lanes:(i + 1) * lanes, 0:lanes] = jnp.where(here, fact_hi[...], 0.0).astype(BF16)
            f_ref[i * lanes:(i + 1) * lanes, lanes:] = jnp.where(here, fact_lo[...], 0.0).astype(BF16)
        tacc[...] += nn_dot(p_ref[block], f_ref[...])

    target = tacc[:, 0:lanes] + tacc[:, lanes:]
    log_index = logit_ref[...] - i_lse
    index_prob = jnp.exp2(log_index)
    positive = target > 0
    log_target = jnp.log(jnp.where(positive, target, 1.0))
    kl = jnp.sum(
        jnp.where(positive, target * (log_target - log_index * math.log(2.0)), 0.0), axis=0, keepdims=True
    )
    dl_ref[0] = loss_scale * (index_prob - target)

    for r in range(1, ZGROUP):
        pltpu.make_async_remote_copy(
            dl_ref.at[0], dl_gather.at[r - 1], send_sem.at[4], zd_sem.at[r - 1],
            device_id=(z_peer(r), pb), device_id_type=MESH,
        ).start()

    kp_ref[...] = jnp.zeros_like(kp_ref)

    @pl.loop(0, pairs // 4)
    def _(step):
        dl = dl_ref[0]
        for u in range(4):
            jp = step * 4 + u
            raw = nt_dot(ik, iq_ref[pl.ds(2 * jp, 2)].reshape(2 * lanes, idim))
            w = wt_ref[pl.ds(2 * jp, 2), :] * iscale
            for h in range(2):
                part = raw[:, h * lanes:(h + 1) * lanes]
                t_send[jp, pl.ds(h, 1), :] = (
                    jnp.sum(dl * jnp.maximum(part, 0.0), axis=0, keepdims=True) * iscale
                )
                coef[:, (2 * u + h) * lanes:(2 * u + h + 1) * lanes] = jnp.where(
                    part > 0, dl * w[h:h + 1], 0.0
                ).astype(BF16)
            t_send[jp, pl.ds(2, 1), :] = kl
            t_send[jp, pl.ds(3, 5), :] = jnp.zeros((5, lanes), F32)
        kp_ref[...] += nn_dot(coef[...], iq_ref[pl.ds(8 * step, 8)].reshape(8 * lanes, idim))

    @pl.loop(1, n_ctx)
    def _(r):
        peer = ctx_peer(r)
        pltpu.make_async_remote_copy(
            t_send.at[peer], t_recv.at[r - 1], send_sem.at[5], recv_sem.at[5],
            device_id=(peer, pb), device_id_type=MESH,
        ).start()

    q_rows = t_rows // n_pb
    for r in range(1, n_pb):
        peer = pb_peer(r)
        pltpu.make_async_remote_copy(
            kp_ref.at[pl.ds(peer * q_rows, q_rows)], kp_recv.at[r - 1], send_sem.at[6], recv_sem.at[6],
            device_id=(ctx, peer), device_id_type=MESH,
        ).start()

    for r in range(1, ZGROUP):
        wait_bytes(dl_gather.at[r - 1], zd_sem.at[r - 1])
        dl_ref[r] = dl_gather[r - 1]

    def query_pair(step):
        k = lax.rem(grp + 1 + step, n_grp)
        jp = k * ZGROUP + z
        iq_pair = iq_ref[pl.ds(2 * jp, 2)].reshape(2 * lanes, idim)
        w = wt_ref[pl.ds(2 * jp, 2), :] * iscale
        for r in range(ZGROUP):
            raw = nt_dot(ik_all[r * t_rows:(r + 1) * t_rows, :], iq_pair)
            dl = dl_ref[r]
            for h in range(2):
                coef2[r * t_rows:(r + 1) * t_rows, h * lanes:(h + 1) * lanes] = jnp.where(
                    raw[:, h * lanes:(h + 1) * lanes] > 0, dl * w[h:h + 1], 0.0
                ).astype(BF16)
        grad = nn_dot(ikt_all[...], coef2[...])
        for h in range(2):
            qs_ref[step, h] = grad[:, h * lanes:(h + 1) * lanes]
        return k

    @pl.loop(0, n_grp - 1)
    def _(step):
        k = query_pair(step)
        pltpu.make_async_remote_copy(
            qs_ref.at[step], q_recv.at[step], send_sem.at[7], recv_sem.at[7],
            device_id=(k * ZGROUP + z, pb), device_id_type=MESH,
        ).start()

    wait_bytes(kp_recv, recv_sem.at[6])
    own_quarter = kp_ref[pl.ds(pb * q_rows, q_rows), :] + kp_recv[0] + kp_recv[1] + kp_recv[2]
    ko_ref[pb] = own_quarter
    for r in range(1, n_pb):
        pltpu.make_async_remote_copy(
            ko_ref.at[pb], ko_ref.at[pb], send_sem.at[8], recv_sem.at[8],
            device_id=(ctx, pb_peer(r)), device_id_type=MESH,
        ).start()

    wait_bytes(t_recv.at[pl.ds(0, n_ctx - 1)], recv_sem.at[5])
    w_total = jnp.sum(t_recv[0:n_ctx - 1], axis=0) + t_send[ctx]
    w_send[...] = w_total
    kl_ref[...] = w_total[2:3, :]

    @pl.loop(1, n_ctx)
    def _(r):
        pltpu.make_async_remote_copy(
            w_send, w_recv.at[ctx], send_sem.at[9], recv_sem.at[9],
            device_id=(ctx_peer(r), pb), device_id_type=MESH,
        ).start()

    query_pair(n_grp - 1)

    wait_bytes(ko_ref.at[pl.ds(0, n_pb - 1)], recv_sem.at[8])
    for i in range(n_pb):
        key_ref[i * q_rows:(i + 1) * q_rows, :] = ko_ref[i]
    wait_bytes(w_recv.at[pl.ds(0, n_ctx - 1)], recv_sem.at[9])
    w_recv[ctx] = w_send[...]
    for i in range(n_ctx):
        wg_ref[2 * i:2 * i + 2, :] = w_recv[i, 0:2, :]

    wait_bytes(q_recv, recv_sem.at[7])
    for h in range(2):
        total = qs_ref[n_grp - 1, h]
        for k in range(n_grp - 1):
            total = total + q_recv[k, h]
        qg_ref[h] = total.T

    wait_bytes(key_gather, send_sem.at[0])
    wait_bytes(ist_recv.at[pl.ds(0, n_ctx - 1)], send_sem.at[1])
    wait_bytes(st_recv.at[pl.ds(0, n_ctx - 1)], send_sem.at[2])
    wait_bytes(lse_recv.at[pl.ds(0, n_ctx - 1)], send_sem.at[3])
    wait_bytes(dl_gather, send_sem.at[4])
    wait_bytes(t_recv.at[pl.ds(0, n_ctx - 1)], send_sem.at[5])
    wait_bytes(kp_recv, send_sem.at[6])
    wait_bytes(q_recv, send_sem.at[7])
    wait_bytes(ko_ref.at[pl.ds(0, n_pb - 1)], send_sem.at[8])
    wait_bytes(w_recv.at[pl.ds(0, n_ctx - 1)], send_sem.at[9])


def local(queries, key_cache, index_queries, index_keys, head_weights, positions, valid_lengths):
    n_ctx, n_pb = lax.axis_size("ctx"), lax.axis_size("pb")
    q_rows, lanes, lat = queries.shape
    t_rows, idim = index_keys.shape
    heads = index_queries.shape[0]
    blocks = q_rows // QBLOCK
    n_grp = n_ctx // ZGROUP
    depth = -(-(lanes + lat) // 256) * 256
    loss_scale = t_rows * n_ctx / (q_rows * n_pb)
    vmem = pltpu.VMEM
    tile = (8, lanes)
    scratch = [
        vmem((2, QBLOCK, depth, lanes), BF16),
        vmem((t_rows, depth), BF16),
        vmem((2, t_rows, 2 * lanes), F32),
        vmem((blocks, t_rows, QBLOCK * lanes), BF16),
        vmem((t_rows, lanes), F32),
        vmem((ZGROUP, t_rows, lanes), F32),
        vmem((q_rows, lanes), F32),
        vmem((lanes, q_rows), F32),
        vmem((lanes, q_rows), F32),
        vmem((QBLOCK * lanes, 2 * lanes), BF16),
        vmem((t_rows, 2 * lanes), F32),
        vmem((idim, ZGROUP * t_rows), BF16),
        vmem((ZGROUP * t_rows, idim), BF16),
        vmem((t_rows, 8 * lanes), BF16),
        vmem((ZGROUP * t_rows, 2 * lanes), BF16),
        vmem((t_rows, idim), F32),
        vmem((ZGROUP - 1, t_rows, idim), F32),
        vmem((ZGROUP - 1, t_rows, lanes), F32),
        vmem(tile, F32),
        vmem((n_ctx, *tile), F32),
        vmem((n_ctx, *tile), F32),
        vmem((n_ctx, *tile), F32),
        vmem(tile, F32),
        vmem((n_ctx, *tile), F32),
        vmem((t_rows, idim), F32),
        vmem((n_pb - 1, t_rows // n_pb, idim), F32),
        vmem((n_pb, t_rows // n_pb, idim), F32),
        vmem((n_ctx, *tile), F32),
        vmem((n_ctx, *tile), F32),
        vmem(tile, F32),
        vmem((n_ctx, *tile), F32),
        vmem((n_grp, 2, idim, lanes), F32),
        vmem((n_grp - 1, 2, idim, lanes), F32),
        pltpu.SemaphoreType.DMA((2,)),
        pltpu.SemaphoreType.DMA((10,)),
        pltpu.SemaphoreType.DMA((10,)),
        pltpu.SemaphoreType.DMA((ZGROUP - 1,)),
        pltpu.SemaphoreType.DMA((ZGROUP - 1,)),
    ]
    on_chip = pl.BlockSpec(memory_space=pltpu.VMEM)
    kl, key_grad, query_grad, weight_grad = pl.pallas_call(
        functools.partial(kernel, n_ctx, n_pb, loss_scale),
        out_shape=(
            jax.ShapeDtypeStruct((1, q_rows), F32),
            jax.ShapeDtypeStruct((t_rows, idim), F32),
            jax.ShapeDtypeStruct((heads // n_ctx, q_rows, idim), F32),
            jax.ShapeDtypeStruct((heads, q_rows), F32),
        ),
        in_specs=[pl.BlockSpec(memory_space=pl.ANY)] + [on_chip] * 6,
        out_specs=(on_chip,) * 4,
        scratch_shapes=scratch,
        compiler_params=pltpu.CompilerParams(
            collective_id=0, has_side_effects=True, vmem_limit_bytes=60 * 1024 * 1024
        ),
    )(
        queries.transpose(0, 2, 1),
        key_cache.T,
        index_queries,
        index_keys,
        head_weights.T,
        positions.reshape(1, q_rows),
        valid_lengths.reshape(1, q_rows),
    )
    return kl.reshape(q_rows), key_grad, query_grad, weight_grad.T


def solution(mesh):
    in_specs = (
        P("pb", None, None),
        P("ctx", None),
        P(None, "pb", None),
        P("ctx", None),
        P("pb", None),
        P("pb"),
        P("pb"),
    )
    out_specs = (P("pb"), P("ctx", None), P("ctx", "pb", None), P("pb", None))
    return jax.shard_map(local, mesh=mesh, in_specs=in_specs, out_specs=out_specs, check_vma=False)
```

```python
import functools
import math

import jax
import jax.numpy as jnp
from jax import lax
from jax.experimental import pallas as pl
from jax.experimental.pallas import tpu as pltpu
from jax.sharding import PartitionSpec as P

NEG = -1e30
LOG2E = math.log2(math.e)
MESH = pl.DeviceIdType.MESH
F32 = jnp.float32
BF16 = jnp.bfloat16
ZGROUP = 4
QBLOCK = 8
OWNED = 4
FIRST = 3


def nt_dot(lhs, rhs):
    return lax.dot_general(lhs, rhs, (((1,), (1,)), ((), ())), preferred_element_type=F32)


def nn_dot(lhs, rhs):
    return jnp.dot(lhs, rhs, preferred_element_type=F32)


def wait_bytes(ref, sem):
    pltpu.make_async_copy(ref, ref, sem).wait()


def kernel(
    n_ctx, n_pb, loss_scale,
    q_hbm, kt_ref, iq_hbm, ik_ref, wt_ref, pos_ref, len_ref,
    kl_ref, key_ref, qg_ref, wg_ref,
    iq_ref, qb, ke, s_ref, peak_ref, p_ref, logit_ref, dl_ref, fac_ref, fact_hi, fact_lo, f_ref, tacc,
    ikt_all, ik_all, coef, coef2,
    key_send, key_gather, dl_gather,
    ist_send, ist_recv, st_send, st_recv, lse_send, lse_recv,
    kp_ref, kp_recv, ko_ref, t_send, t_recv, w_send, w_recv, qs_ref, q_recv,
    iq_sem, q_sem, send_sem, recv_sem, zk_sem, zd_sem,
    st_ssem, st_rsem, lse_ssem, lse_rsem,
):
    ctx = lax.axis_index("ctx")
    pb = lax.axis_index("pb")
    z = lax.rem(ctx, ZGROUP)
    grp = ctx // ZGROUP
    n_grp = n_ctx // ZGROUP
    heads = iq_ref.shape[0]
    pairs = heads // 2
    _, _, lat, lanes = q_hbm.shape
    queries = OWNED * n_ctx
    t_rows = ik_ref.shape[0]
    idim = ik_ref.shape[1]
    blocks = queries // QBLOCK
    iscale = idim ** -0.5
    mscale = 192 ** -0.5 * LOG2E

    def ctx_peer(r):
        return lax.rem(ctx + r, n_ctx)

    def pb_peer(r):
        return lax.rem(pb + r, n_pb)

    def z_peer(r):
        return grp * ZGROUP + lax.rem(z + r, ZGROUP)

    barrier = pltpu.get_barrier_semaphore()

    @pl.loop(1, n_ctx)
    def _(r):
        pl.semaphore_signal(barrier, inc=1, device_id=(ctx_peer(r), pb), device_id_type=MESH)

    @pl.loop(1, n_pb)
    def _(r):
        pl.semaphore_signal(barrier, inc=1, device_id=(ctx, pb_peer(r)), device_id_type=MESH)

    per_row = n_ctx // QBLOCK

    def first_query(block):
        return OWNED * QBLOCK * lax.rem(block, per_row) + block // per_row

    def q_copy(block, slot):
        return pltpu.make_async_copy(
            q_hbm.at[pl.ds(QBLOCK * lax.rem(block, per_row), QBLOCK), block // per_row],
            qb.at[slot, :, pl.ds(lanes, lat), :],
            q_sem.at[slot],
        )

    q_copy(0, 0).start()
    q_copy(1, 1).start()
    iq_copy = pltpu.make_async_copy(iq_hbm, iq_ref, iq_sem)
    iq_copy.start()

    t_index = ctx * t_rows + lax.broadcasted_iota(jnp.int32, (t_rows, lanes), 0)
    pos = pos_ref[...]
    visible = (t_index <= pos) & (t_index > pos - len_ref[...])
    bias = jnp.where(visible, 0.0, NEG)
    ke[:, 0:lanes] = bias.astype(BF16)
    ke[:, lanes:lanes + lat] = kt_ref[...].astype(F32).T.astype(BF16)
    depth = ke.shape[1]
    pad = depth - lanes - lat
    ke[:, lanes + lat:] = jnp.zeros((t_rows, pad), BF16)
    for slot in range(2):
        for i in range(QBLOCK):
            qb[slot, i, lanes + lat:, :] = jnp.zeros((pad, lanes), BF16)

    ik = ik_ref[...]
    key_send[...] = ik.astype(F32)

    pl.semaphore_wait(barrier, n_ctx - 1 + n_pb - 1)

    for r in range(1, ZGROUP):
        pltpu.make_async_remote_copy(
            key_send, key_gather.at[r - 1], send_sem.at[0], zk_sem.at[r - 1],
            device_id=(z_peer(r), pb), device_id_type=MESH,
        ).start()

    st_send[...] = jnp.zeros_like(st_send)

    def exponentials(block):
        row = block // per_row
        part = row // FIRST
        for u in range(QBLOCK // 2):
            peak = peak_ref[u:u + 1, :]
            expo = jnp.exp2(s_ref[:, 2 * u * lanes:(2 * u + 2) * lanes] * mscale - peak)
            total = jnp.sum(expo, axis=0, keepdims=True)
            p_ref[block, :, 2 * u * lanes:(2 * u + 2) * lanes] = expo.astype(BF16)
            for h in range(2):
                owner = QBLOCK * lax.rem(block, per_row) + 2 * u + h
                st_send[part, owner, pl.ds(row, 1), :] = peak[:, h * lanes:(h + 1) * lanes]
                st_send[part, owner, pl.ds(OWNED + row, 1), :] = total[:, h * lanes:(h + 1) * lanes]

    def scores(block):
        slot = lax.rem(block, 2)
        q_copy(block, slot).wait()
        row = lax.broadcasted_iota(jnp.int32, (lanes, lanes), 0)
        first = first_query(block)
        for i in range(QBLOCK):
            qb[slot, i, 0:lanes, :] = jnp.where(row == first + OWNED * i, 1.0, 0.0).astype(BF16)
        exponentials(lax.max(block - 1, 0))
        rhs = jnp.concatenate([qb[slot, i] for i in range(QBLOCK)], axis=1)
        s = nn_dot(ke[...], rhs)
        s_ref[...] = s
        peak = jnp.max(s, axis=0, keepdims=True) * mscale
        for u in range(QBLOCK // 2):
            peak_ref[u:u + 1, :] = peak[:, 2 * u * lanes:(2 * u + 2) * lanes]

        @pl.when(block + 2 < blocks)
        def _():
            q_copy(block + 2, slot).start()

    def send_stats(part):
        @pl.loop(1, n_ctx)
        def _(r):
            peer = ctx_peer(r)
            pltpu.make_async_remote_copy(
                st_send.at[part, peer], st_recv.at[part, r - 1], st_ssem.at[part], st_rsem.at[part],
                device_id=(peer, pb), device_id_type=MESH,
            ).start()

    def combine(part):
        wait_bytes(st_recv.at[part, pl.ds(0, n_ctx - 1)], st_rsem.at[part])
        st_recv[part, n_ctx - 1] = st_send[part, ctx]
        got = st_recv[part]
        peaks, sums = got[:, 0:OWNED, :], got[:, OWNED:, :]
        top = jnp.max(peaks, axis=0)
        total = jnp.sum(sums * jnp.exp2(peaks - top[None]), axis=0)
        lse_send[part] = jnp.zeros((2 * OWNED, lanes), F32)
        lse_send[part, 0:OWNED, :] = top + jnp.log(jnp.maximum(total, 1e-30)) * LOG2E

        @pl.loop(1, n_ctx)
        def _(r):
            pltpu.make_async_remote_copy(
                lse_send.at[part], lse_recv.at[part, ctx], lse_ssem.at[part], lse_rsem.at[part],
                device_id=(ctx_peer(r), pb), device_id_type=MESH,
            ).start()

    def factors(part):
        wait_bytes(lse_recv.at[part, pl.ds(0, n_ctx - 1)], lse_rsem.at[part])
        lse_recv[part, ctx] = lse_send[part]
        for i in range(n_ctx):
            fac_ref[OWNED * i:OWNED * (i + 1), :] = jnp.exp2(
                st_send[part, i, 0:OWNED, :] - lse_recv[part, i, 0:OWNED, :]
            )
        fact = fac_ref[...].T * (1.0 / lanes)
        hi = fact.astype(BF16)
        fact_hi[...] = hi.astype(F32)
        fact_lo[...] = fact - hi.astype(F32)

    split = FIRST * per_row

    @pl.loop(0, split + 1)
    def _(block):
        scores(block)

    send_stats(0)

    @pl.loop(split + 1, blocks)
    def _(block):
        scores(block)

    exponentials(blocks - 1)
    send_stats(1)
    combine(0)

    iq_copy.wait()
    logit_ref[...] = jnp.zeros_like(logit_ref)

    @pl.loop(0, pairs // 4)
    def _(step):
        total = logit_ref[...]
        for u in range(4):
            jp = step * 4 + u
            raw = nt_dot(ik, iq_ref[pl.ds(2 * jp, 2)].reshape(2 * lanes, idim))
            w = wt_ref[pl.ds(2 * jp, 2), :]
            total = total + jnp.maximum(raw[:, :lanes], 0.0) * w[0:1]
            total = total + jnp.maximum(raw[:, lanes:], 0.0) * w[1:2]
        logit_ref[...] = total

    logits = logit_ref[...] * (iscale * LOG2E) + bias
    logit_ref[...] = logits
    i_peak = jnp.max(logits, axis=0, keepdims=True)
    i_sum = jnp.sum(jnp.exp2(logits - i_peak), axis=0, keepdims=True)
    ist_send[...] = jnp.zeros_like(ist_send)
    ist_send[0:1, :] = i_peak
    ist_send[1:2, :] = i_sum

    @pl.loop(1, n_ctx)
    def _(r):
        pltpu.make_async_remote_copy(
            ist_send, ist_recv.at[r - 1], send_sem.at[1], recv_sem.at[1],
            device_id=(ctx_peer(r), pb), device_id_type=MESH,
        ).start()

    ik_all[0:t_rows, :] = ik
    ikt_all[:, 0:t_rows] = key_send[...].T.astype(BF16)
    for r in range(1, ZGROUP):
        wait_bytes(key_gather.at[r - 1], zk_sem.at[r - 1])
        got = key_gather[r - 1]
        ik_all[r * t_rows:(r + 1) * t_rows, :] = got.astype(BF16)
        ikt_all[:, r * t_rows:(r + 1) * t_rows] = got.T.astype(BF16)

    combine(1)
    tacc[...] = jnp.zeros_like(tacc)

    def add_target(block):
        lane = lax.broadcasted_iota(jnp.int32, (lanes, lanes), 1)
        first = first_query(block)
        for i in range(QBLOCK):
            here = lane == first + OWNED * i
            f_ref[i * lanes:(i + 1) * lanes, 0:lanes] = jnp.where(here, fact_hi[...], 0.0).astype(BF16)
            f_ref[i * lanes:(i + 1) * lanes, lanes:] = jnp.where(here, fact_lo[...], 0.0).astype(BF16)
        tacc[...] += nn_dot(p_ref[block], f_ref[...])

    factors(0)

    @pl.loop(0, split)
    def _(block):
        add_target(block)

    factors(1)

    @pl.loop(split, blocks)
    def _(block):
        add_target(block)

    wait_bytes(ist_recv.at[pl.ds(0, n_ctx - 1)], recv_sem.at[1])
    ist_recv[n_ctx - 1] = ist_send[...]
    got = ist_recv[...]
    peaks, sums = got[:, 0:1, :], got[:, 1:2, :]
    top = jnp.max(peaks, axis=0)
    i_lse = top + jnp.log(jnp.sum(sums * jnp.exp2(peaks - top[None]), axis=0)) * LOG2E

    target = tacc[:, 0:lanes] + tacc[:, lanes:]
    log_index = logit_ref[...] - i_lse
    index_prob = jnp.exp2(log_index)
    positive = target > 0
    log_target = jnp.log(jnp.where(positive, target, 1.0))
    kl = jnp.sum(
        jnp.where(positive, target * (log_target - log_index * math.log(2.0)), 0.0), axis=0, keepdims=True
    )
    dl_ref[0] = loss_scale * (index_prob - target)

    for r in range(1, ZGROUP):
        pltpu.make_async_remote_copy(
            dl_ref.at[0], dl_gather.at[r - 1], send_sem.at[4], zd_sem.at[r - 1],
            device_id=(z_peer(r), pb), device_id_type=MESH,
        ).start()

    kp_ref[...] = jnp.zeros_like(kp_ref)

    @pl.loop(0, pairs // 4)
    def _(step):
        dl = dl_ref[0]
        for u in range(4):
            jp = step * 4 + u
            raw = nt_dot(ik, iq_ref[pl.ds(2 * jp, 2)].reshape(2 * lanes, idim))
            w = wt_ref[pl.ds(2 * jp, 2), :] * iscale
            for h in range(2):
                part = raw[:, h * lanes:(h + 1) * lanes]
                t_send[jp, pl.ds(h, 1), :] = (
                    jnp.sum(dl * jnp.maximum(part, 0.0), axis=0, keepdims=True) * iscale
                )
                coef[:, (2 * u + h) * lanes:(2 * u + h + 1) * lanes] = jnp.where(
                    part > 0, dl * w[h:h + 1], 0.0
                ).astype(BF16)
            t_send[jp, pl.ds(2, 1), :] = kl
            t_send[jp, pl.ds(3, 5), :] = jnp.zeros((5, lanes), F32)
        kp_ref[...] += nn_dot(coef[...], iq_ref[pl.ds(8 * step, 8)].reshape(8 * lanes, idim))

    @pl.loop(1, n_ctx)
    def _(r):
        peer = ctx_peer(r)
        pltpu.make_async_remote_copy(
            t_send.at[peer], t_recv.at[r - 1], send_sem.at[5], recv_sem.at[5],
            device_id=(peer, pb), device_id_type=MESH,
        ).start()

    q_rows = t_rows // n_pb
    for r in range(1, n_pb):
        peer = pb_peer(r)
        pltpu.make_async_remote_copy(
            kp_ref.at[pl.ds(peer * q_rows, q_rows)], kp_recv.at[r - 1], send_sem.at[6], recv_sem.at[6],
            device_id=(ctx, peer), device_id_type=MESH,
        ).start()

    wait_bytes(t_recv.at[pl.ds(0, n_ctx - 1)], recv_sem.at[5])
    w_total = jnp.sum(t_recv[0:n_ctx - 1], axis=0) + t_send[ctx]
    w_send[...] = w_total
    kl_ref[...] = w_total[2:3, :]

    @pl.loop(1, n_ctx)
    def _(r):
        pltpu.make_async_remote_copy(
            w_send, w_recv.at[ctx], send_sem.at[9], recv_sem.at[9],
            device_id=(ctx_peer(r), pb), device_id_type=MESH,
        ).start()

    wait_bytes(kp_recv, recv_sem.at[6])
    own_quarter = kp_ref[pl.ds(pb * q_rows, q_rows), :] + kp_recv[0] + kp_recv[1] + kp_recv[2]
    ko_ref[pb] = own_quarter
    for r in range(1, n_pb):
        pltpu.make_async_remote_copy(
            ko_ref.at[pb], ko_ref.at[pb], send_sem.at[8], recv_sem.at[8],
            device_id=(ctx, pb_peer(r)), device_id_type=MESH,
        ).start()

    for r in range(1, ZGROUP):
        wait_bytes(dl_gather.at[r - 1], zd_sem.at[r - 1])
        dl_ref[r] = dl_gather[r - 1]

    def query_pair(step):
        k = lax.rem(grp + 1 + step, n_grp)
        jp = k * ZGROUP + z
        iq_pair = iq_ref[pl.ds(2 * jp, 2)].reshape(2 * lanes, idim)
        w = wt_ref[pl.ds(2 * jp, 2), :] * iscale
        for r in range(ZGROUP):
            raw = nt_dot(ik_all[r * t_rows:(r + 1) * t_rows, :], iq_pair)
            dl = dl_ref[r]
            for h in range(2):
                coef2[r * t_rows:(r + 1) * t_rows, h * lanes:(h + 1) * lanes] = jnp.where(
                    raw[:, h * lanes:(h + 1) * lanes] > 0, dl * w[h:h + 1], 0.0
                ).astype(BF16)
        grad = nn_dot(ikt_all[...], coef2[...])
        for h in range(2):
            qs_ref[step, h] = grad[:, h * lanes:(h + 1) * lanes]
        return k

    @pl.loop(0, n_grp - 1)
    def _(step):
        k = query_pair(step)
        pltpu.make_async_remote_copy(
            qs_ref.at[step], q_recv.at[step], send_sem.at[7], recv_sem.at[7],
            device_id=(k * ZGROUP + z, pb), device_id_type=MESH,
        ).start()

    query_pair(n_grp - 1)

    wait_bytes(ko_ref.at[pl.ds(0, n_pb - 1)], recv_sem.at[8])
    for i in range(n_pb):
        key_ref[i * q_rows:(i + 1) * q_rows, :] = ko_ref[i]
    wait_bytes(w_recv.at[pl.ds(0, n_ctx - 1)], recv_sem.at[9])
    w_recv[ctx] = w_send[...]
    for i in range(n_ctx):
        wg_ref[2 * i:2 * i + 2, :] = w_recv[i, 0:2, :]

    wait_bytes(q_recv, recv_sem.at[7])
    for h in range(2):
        total = qs_ref[n_grp - 1, h]
        for k in range(n_grp - 1):
            total = total + q_recv[k, h]
        qg_ref[h] = total.T

    wait_bytes(key_gather, send_sem.at[0])
    wait_bytes(ist_recv.at[pl.ds(0, n_ctx - 1)], send_sem.at[1])
    for part in range(2):
        wait_bytes(st_recv.at[part, pl.ds(0, n_ctx - 1)], st_ssem.at[part])
        wait_bytes(lse_recv.at[part, pl.ds(0, n_ctx - 1)], lse_ssem.at[part])
    wait_bytes(dl_gather, send_sem.at[4])
    wait_bytes(t_recv.at[pl.ds(0, n_ctx - 1)], send_sem.at[5])
    wait_bytes(kp_recv, send_sem.at[6])
    wait_bytes(q_recv, send_sem.at[7])
    wait_bytes(ko_ref.at[pl.ds(0, n_pb - 1)], send_sem.at[8])
    wait_bytes(w_recv.at[pl.ds(0, n_ctx - 1)], send_sem.at[9])


def hand_on(*refs):
    for source, target in zip(refs[:4], refs[4:]):
        target[...] = source[...]


def local(queries, key_cache, index_queries, index_keys, head_weights, positions, valid_lengths):
    n_ctx, n_pb = lax.axis_size("ctx"), lax.axis_size("pb")
    q_rows, lanes, lat = queries.shape
    t_rows, idim = index_keys.shape
    heads = index_queries.shape[0]
    blocks = q_rows // QBLOCK
    n_grp = n_ctx // ZGROUP
    depth = -(-(lanes + lat) // 256) * 256
    loss_scale = t_rows * n_ctx / (q_rows * n_pb)
    vmem = pltpu.VMEM
    tile = (8, lanes)
    scratch = [
        vmem((heads, q_rows, idim), BF16),
        vmem((2, QBLOCK, depth, lanes), BF16),
        vmem((t_rows, depth), BF16),
        vmem((t_rows, QBLOCK * lanes), F32),
        vmem((8, 2 * lanes), F32),
        vmem((blocks, t_rows, QBLOCK * lanes), BF16),
        vmem((t_rows, lanes), F32),
        vmem((ZGROUP, t_rows, lanes), F32),
        vmem((q_rows, lanes), F32),
        vmem((lanes, q_rows), F32),
        vmem((lanes, q_rows), F32),
        vmem((QBLOCK * lanes, 2 * lanes), BF16),
        vmem((t_rows, 2 * lanes), F32),
        vmem((idim, ZGROUP * t_rows), BF16),
        vmem((ZGROUP * t_rows, idim), BF16),
        vmem((t_rows, 8 * lanes), BF16),
        vmem((ZGROUP * t_rows, 2 * lanes), BF16),
        vmem((t_rows, idim), F32),
        vmem((ZGROUP - 1, t_rows, idim), F32),
        vmem((ZGROUP - 1, t_rows, lanes), F32),
        vmem(tile, F32),
        vmem((n_ctx, *tile), F32),
        vmem((2, n_ctx, *tile), F32),
        vmem((2, n_ctx, *tile), F32),
        vmem((2, *tile), F32),
        vmem((2, n_ctx, *tile), F32),
        vmem((t_rows, idim), F32),
        vmem((n_pb - 1, t_rows // n_pb, idim), F32),
        vmem((n_pb, t_rows // n_pb, idim), F32),
        vmem((n_ctx, *tile), F32),
        vmem((n_ctx, *tile), F32),
        vmem(tile, F32),
        vmem((n_ctx, *tile), F32),
        vmem((n_grp, 2, idim, lanes), F32),
        vmem((n_grp - 1, 2, idim, lanes), F32),
        pltpu.SemaphoreType.DMA,
        pltpu.SemaphoreType.DMA((2,)),
        pltpu.SemaphoreType.DMA((10,)),
        pltpu.SemaphoreType.DMA((10,)),
        pltpu.SemaphoreType.DMA((ZGROUP - 1,)),
        pltpu.SemaphoreType.DMA((ZGROUP - 1,)),
    ] + [pltpu.SemaphoreType.DMA((2,))] * 4
    on_chip = pl.BlockSpec(memory_space=pltpu.VMEM)
    in_hbm = pl.BlockSpec(memory_space=pl.ANY)
    results = pl.pallas_call(
        functools.partial(kernel, n_ctx, n_pb, loss_scale),
        out_shape=(
            jax.ShapeDtypeStruct((1, q_rows), F32),
            jax.ShapeDtypeStruct((t_rows, idim), F32),
            jax.ShapeDtypeStruct((heads // n_ctx, q_rows, idim), F32),
            jax.ShapeDtypeStruct((heads, q_rows), F32),
        ),
        in_specs=[in_hbm, on_chip, in_hbm] + [on_chip] * 4,
        out_specs=(on_chip,) * 4,
        scratch_shapes=scratch,
        compiler_params=pltpu.CompilerParams(
            collective_id=0, has_side_effects=True, vmem_limit_bytes=60 * 1024 * 1024
        ),
    )(
        queries.transpose(0, 2, 1).reshape(n_ctx, OWNED, lat, lanes),
        key_cache.T,
        index_queries,
        index_keys,
        head_weights.T,
        positions.reshape(1, q_rows),
        valid_lengths.reshape(1, q_rows),
    )
    kl, key_grad, query_grad, weight_grad = pl.pallas_call(
        hand_on,
        out_shape=tuple(jax.ShapeDtypeStruct(x.shape, x.dtype) for x in results),
        in_specs=[on_chip] * 4,
        out_specs=(on_chip,) * 4,
    )(*results)
    return kl.reshape(q_rows), key_grad, query_grad, weight_grad.T


def solution(mesh):
    in_specs = (
        P("pb", None, None),
        P("ctx", None),
        P(None, "pb", None),
        P("ctx", None),
        P("pb", None),
        P("pb"),
        P("pb"),
    )
    out_specs = (P("pb"), P("ctx", None), P("ctx", "pb", None), P("pb", None))
    return jax.shard_map(local, mesh=mesh, in_specs=in_specs, out_specs=out_specs, check_vma=False)
```

```python
import functools
import math

import jax
import jax.numpy as jnp
from jax import lax
from jax.experimental import pallas as pl
from jax.experimental.pallas import tpu as pltpu
from jax.sharding import PartitionSpec as P

NEG = -1e30
LOG2E = math.log2(math.e)
MESH = pl.DeviceIdType.MESH
F32 = jnp.float32
BF16 = jnp.bfloat16
ZGROUP = 4
QBLOCK = 8
KSPLIT = 5
TSTEP = 4
OWNED = 2


def nt_dot(lhs, rhs):
    return lax.dot_general(lhs, rhs, (((1,), (1,)), ((), ())), preferred_element_type=F32)


def nn_dot(lhs, rhs):
    return jnp.dot(lhs, rhs, preferred_element_type=F32)


def wait_bytes(ref, sem):
    pltpu.make_async_copy(ref, ref, sem).wait()


def kernel(
    n_ctx, n_pb, loss_scale,
    q_hbm, kt_hbm, iq_hbm, ik_ref, wt_ref, pos_ref, len_ref,
    kl_ref, key_ref, qg_ref, wg_ref,
    iq_ref, kt_ref, qb, ke, s_ref, peak_ref, p_ref, logit_ref, dl_ref, fac_ref, fact_hi, fact_lo, f_ref, tacc,
    ikt_all, ik_all, coef, coef2, w2_ref, relu_ref,
    key_send, key_gather, dl_send, dl_gather, dl_twice,
    ist_send, ist_recv, st_send, st_recv, lse_send, lse_recv,
    kp_ref, kc_ref, kh_ref, ko_ref, t_send, t_recv, w_send, w_recv, qs_ref, q_recv,
    iq_sem, kt_sem, q_sem, send_sem, recv_sem, zk_sem, zd_sem,
    st_ssem, st_rsem, lse_ssem, lse_rsem, zd_ssem, qr_ssem, qr_rsem, kp_ssem, kp_rsem,
):
    ctx = lax.axis_index("ctx")
    pb = lax.axis_index("pb")
    z = lax.rem(ctx, ZGROUP)
    grp = ctx // ZGROUP
    n_grp = n_ctx // ZGROUP
    heads = iq_ref.shape[0]
    pairs = heads // 2
    queries, lat, lanes = q_hbm.shape
    half_lanes = lanes // 2
    half_rows = ik_ref.shape[0] // 2
    t_rows = ik_ref.shape[0]
    idim = ik_ref.shape[1]
    blocks = queries // QBLOCK
    split = blocks // 2
    iscale = idim ** -0.5
    mscale = 192 ** -0.5 * LOG2E

    def ctx_peer(r):
        return lax.rem(ctx + r, n_ctx)

    def pb_peer(r):
        return lax.rem(pb + r, n_pb)

    def z_peer(r):
        return grp * ZGROUP + lax.rem(z + r, ZGROUP)

    def q_copy(block, slot):
        return pltpu.make_async_copy(
            q_hbm.at[pl.ds(block * QBLOCK, QBLOCK)],
            qb.at[slot, :, pl.ds(0, lat), :],
            q_sem.at[slot],
        )

    kt_copy = pltpu.make_async_copy(kt_hbm, kt_ref, kt_sem)
    kt_copy.start()
    q_copy(0, 0).start()
    q_copy(1, 1).start()
    iq_copy = pltpu.make_async_copy(iq_hbm, iq_ref, iq_sem)
    iq_copy.start()

    barrier = pltpu.get_barrier_semaphore()

    @pl.loop(1, n_ctx)
    def _(r):
        pl.semaphore_signal(barrier, inc=1, device_id=(ctx_peer(r), pb), device_id_type=MESH)

    @pl.loop(1, n_pb)
    def _(r):
        pl.semaphore_signal(barrier, inc=1, device_id=(ctx, pb_peer(r)), device_id_type=MESH)

    t_index = ctx * t_rows + lax.broadcasted_iota(jnp.int32, (t_rows, lanes), 0)
    pos = pos_ref[...]
    visible = (t_index <= pos) & (t_index > pos - len_ref[...])
    bias = jnp.where(visible, 0.0, NEG)
    hidden = ke.shape[1] - lanes
    kt_copy.wait()
    ke[:, 0:lat] = kt_ref[...].astype(F32).T.astype(BF16)
    ke[:, lat:hidden] = jnp.zeros((t_rows, hidden - lat), BF16)
    ke[:, hidden:] = bias.astype(BF16)
    for slot in range(2):
        for i in range(QBLOCK):
            qb[slot, i, lat:hidden, :] = jnp.zeros((hidden - lat, lanes), BF16)

    w_even = wt_ref[pl.ds(0, pairs, stride=2), :] * iscale
    w_odd = wt_ref[pl.ds(1, pairs, stride=2), :] * iscale
    first_lanes = lax.broadcasted_iota(jnp.int32, (pairs, lanes), 1) < half_lanes
    w2_ref[0] = jnp.where(first_lanes, w_even, pltpu.roll(w_odd, half_lanes, 1))
    w2_ref[1] = jnp.where(first_lanes, pltpu.roll(w_even, half_lanes, 1), w_odd)

    ik = ik_ref[...]
    key_send[...] = ik.astype(F32)

    pl.semaphore_wait(barrier, n_ctx - 1 + n_pb - 1)

    for r in range(1, ZGROUP):
        pltpu.make_async_remote_copy(
            key_send, key_gather.at[r - 1], send_sem.at[0], zk_sem.at[r - 1],
            device_id=(z_peer(r), pb), device_id_type=MESH,
        ).start()

    st_send[...] = jnp.zeros_like(st_send)

    def exponentials(block):
        part = block // split
        for u in range(QBLOCK // 2):
            peak = peak_ref[u:u + 1, :]
            expo = jnp.exp2(s_ref[:, 2 * u * lanes:(2 * u + 2) * lanes] * mscale - peak)
            total = jnp.sum(expo, axis=0, keepdims=True)
            p_ref[block, :, 2 * u * lanes:(2 * u + 2) * lanes] = expo.astype(BF16)
            for h in range(2):
                i = 2 * u + h
                owner = QBLOCK // OWNED * lax.rem(block, split) + i // OWNED
                st_send[part, owner, pl.ds(i % OWNED, 1), :] = peak[:, h * lanes:(h + 1) * lanes]
                st_send[part, owner, pl.ds(4 + i % OWNED, 1), :] = total[:, h * lanes:(h + 1) * lanes]

    def scores(block):
        slot = lax.rem(block, 2)
        q_copy(block, slot).wait()
        row = lax.broadcasted_iota(jnp.int32, (lanes, lanes), 0)
        for i in range(QBLOCK):
            qb[slot, i, hidden:, :] = jnp.where(row == block * QBLOCK + i, 1.0, 0.0).astype(BF16)
        exponentials(lax.max(block - 1, 0))
        rhs = jnp.concatenate([qb[slot, i] for i in range(QBLOCK)], axis=1)
        s = nn_dot(ke[...], rhs)
        s_ref[...] = s
        peak = jnp.max(s, axis=0, keepdims=True) * mscale
        for u in range(QBLOCK // 2):
            peak_ref[u:u + 1, :] = peak[:, 2 * u * lanes:(2 * u + 2) * lanes]

        @pl.when(block + 2 < blocks)
        def _():
            q_copy(block + 2, slot).start()

    def send_stats(part):
        @pl.loop(1, n_ctx)
        def _(r):
            peer = ctx_peer(r)
            pltpu.make_async_remote_copy(
                st_send.at[part, peer], st_recv.at[part, r - 1], st_ssem.at[part], st_rsem.at[part],
                device_id=(peer, pb), device_id_type=MESH,
            ).start()

    def combine(part):
        wait_bytes(st_recv.at[part, pl.ds(0, n_ctx - 1)], st_rsem.at[part])
        st_recv[part, n_ctx - 1] = st_send[part, ctx]
        got = st_recv[part]
        peaks, sums = got[:, 0:4, :], got[:, 4:8, :]
        top = jnp.max(peaks, axis=0)
        total = jnp.sum(sums * jnp.exp2(peaks - top[None]), axis=0)
        lse_send[part] = jnp.zeros((8, lanes), F32)
        lse_send[part, 0:4, :] = top + jnp.log(jnp.maximum(total, 1e-30)) * LOG2E

        @pl.loop(1, n_ctx)
        def _(r):
            pltpu.make_async_remote_copy(
                lse_send.at[part], lse_recv.at[part, ctx], lse_ssem.at[part], lse_rsem.at[part],
                device_id=(ctx_peer(r), pb), device_id_type=MESH,
            ).start()

    def factors(part):
        wait_bytes(lse_recv.at[part, pl.ds(0, n_ctx - 1)], lse_rsem.at[part])
        lse_recv[part, ctx] = lse_send[part]
        for i in range(n_ctx):
            row = part * OWNED * n_ctx + OWNED * i
            fac_ref[row:row + OWNED, :] = jnp.exp2(
                st_send[part, i, 0:OWNED, :] - lse_recv[part, i, 0:OWNED, :]
            )
        fact = fac_ref[...].T * (1.0 / lanes)
        hi = fact.astype(BF16)
        fact_hi[...] = hi.astype(F32)
        fact_lo[...] = fact - hi.astype(F32)

    @pl.loop(0, split + 1)
    def _(block):
        scores(block)

    send_stats(0)

    @pl.loop(split + 1, blocks)
    def _(block):
        scores(block)

    exponentials(blocks - 1)
    send_stats(1)
    combine(0)

    iq_copy.wait()
    logit_ref[...] = jnp.zeros_like(logit_ref)

    @pl.loop(0, pairs // 4)
    def _(step):
        total = logit_ref[...]
        for u in range(4):
            jp = step * 4 + u
            raw = nt_dot(ik, iq_ref[pl.ds(2 * jp, 2)].reshape(2 * lanes, idim))
            w = wt_ref[pl.ds(2 * jp, 2), :]
            active = jnp.maximum(raw, 0.0)
            relu_ref[jp] = active
            total = total + active[:, :lanes] * w[0:1]
            total = total + active[:, lanes:] * w[1:2]
        logit_ref[...] = total

    logits = logit_ref[...] * (iscale * LOG2E) + bias
    logit_ref[...] = logits
    i_peak = jnp.max(logits, axis=0, keepdims=True)
    i_sum = jnp.sum(jnp.exp2(logits - i_peak), axis=0, keepdims=True)
    ist_send[...] = jnp.zeros_like(ist_send)
    ist_send[0:1, :] = i_peak
    ist_send[1:2, :] = i_sum

    @pl.loop(1, n_ctx)
    def _(r):
        pltpu.make_async_remote_copy(
            ist_send, ist_recv.at[r - 1], send_sem.at[1], recv_sem.at[1],
            device_id=(ctx_peer(r), pb), device_id_type=MESH,
        ).start()

    combine(1)

    ik_all[0:t_rows, :] = ik
    ikt_all[:, 0:t_rows] = key_send[...].T.astype(BF16)
    for r in range(1, ZGROUP):
        wait_bytes(key_gather.at[r - 1], zk_sem.at[r - 1])
        got = key_gather[r - 1]
        ik_all[r * t_rows:(r + 1) * t_rows, :] = got.astype(BF16)
        ikt_all[:, r * t_rows:(r + 1) * t_rows] = got.T.astype(BF16)

    tacc[...] = jnp.zeros_like(tacc)

    def add_target(step):
        lane = lax.broadcasted_iota(jnp.int32, (lanes, lanes), 1)
        for i in range(TSTEP * QBLOCK):
            here = lane == step * (TSTEP * QBLOCK) + i
            f_ref[i * lanes:(i + 1) * lanes, 0:lanes] = jnp.where(here, fact_hi[...], 0.0).astype(BF16)
            f_ref[i * lanes:(i + 1) * lanes, lanes:] = jnp.where(here, fact_lo[...], 0.0).astype(BF16)
        wide = jnp.concatenate([p_ref[TSTEP * step + u] for u in range(TSTEP)], axis=1)
        tacc[...] += nn_dot(wide, f_ref[...])

    lower = lax.broadcasted_iota(jnp.int32, (half_rows, lanes), 1) < half_lanes

    def swap(x):
        return pltpu.roll(x, half_lanes, 1)

    def send_dlogit(half, dl):
        top, bottom = dl[:half_rows], dl[half_rows:]
        if half == 0:
            dl_send[half] = jnp.where(lower, top, swap(bottom))
        else:
            dl_send[half] = jnp.where(lower, swap(top), bottom)
        for r in range(1, ZGROUP):
            pltpu.make_async_remote_copy(
                dl_send.at[half], dl_gather.at[half, r - 1], zd_ssem.at[half], zd_sem.at[half, r - 1],
                device_id=(z_peer(r), pb), device_id_type=MESH,
            ).start()

    factors(0)

    @pl.loop(0, split // TSTEP)
    def _(step):
        add_target(step)

    wait_bytes(ist_recv.at[pl.ds(0, n_ctx - 1)], recv_sem.at[1])
    ist_recv[n_ctx - 1] = ist_send[...]
    got = ist_recv[...]
    peaks, sums = got[:, 0:1, :], got[:, 1:2, :]
    top = jnp.max(peaks, axis=0)
    i_lse = top + jnp.log(jnp.sum(sums * jnp.exp2(peaks - top[None]), axis=0)) * LOG2E

    index_prob = jnp.exp2(logit_ref[...] - i_lse)
    send_dlogit(0, loss_scale * (index_prob - (tacc[:, 0:lanes] + tacc[:, lanes:])))

    factors(1)

    @pl.loop(split // TSTEP, blocks // TSTEP)
    def _(step):
        add_target(step)

    target = tacc[:, 0:lanes] + tacc[:, lanes:]
    log_index = logit_ref[...] - i_lse
    index_prob = jnp.exp2(log_index)
    dl_ref[...] = loss_scale * (index_prob - target)
    send_dlogit(1, dl_ref[...])
    positive = target > 0
    log_target = jnp.log(jnp.where(positive, target, 1.0))
    kl = jnp.sum(
        jnp.where(positive, target * (log_target - log_index * math.log(2.0)), 0.0), axis=0, keepdims=True
    )

    kp_ref[...] = jnp.zeros_like(kp_ref)

    def key_step(step):
        dl = dl_ref[...]
        for u in range(4):
            jp = step * 4 + u
            w = wt_ref[pl.ds(2 * jp, 2), :] * iscale
            for h in range(2):
                part = relu_ref[jp, :, h * lanes:(h + 1) * lanes]
                t_send[jp, pl.ds(h, 1), :] = jnp.sum(dl * part, axis=0, keepdims=True) * iscale
                coef[:, (2 * u + h) * lanes:(2 * u + h + 1) * lanes] = jnp.where(
                    part > 0, dl * w[h:h + 1], 0.0
                ).astype(BF16)
            t_send[jp, pl.ds(2, 1), :] = kl
            t_send[jp, pl.ds(3, 5), :] = jnp.zeros((5, lanes), F32)
        kp_ref[...] += nn_dot(coef[...], iq_ref[pl.ds(8 * step, 8)].reshape(8 * lanes, idim))

    @pl.loop(0, KSPLIT)
    def _(step):
        key_step(step)

    def query_half(half, between):
        for r in range(ZGROUP):
            if r:
                wait_bytes(dl_gather.at[half, r - 1], zd_sem.at[half, r - 1])
            packed = dl_gather[half, r - 1] if r else dl_send[half]
            other = swap(packed)
            dl_twice[r, 0:half_rows, :] = jnp.where(lower, packed, other)
            dl_twice[r, half_rows:, :] = jnp.where(lower, other, packed)

        def share(k):
            return k * ZGROUP + z

        def iq_half(k):
            part = iq_ref[pl.ds(2 * share(k), 2), half * half_lanes:(half + 1) * half_lanes, :]
            return part.reshape(lanes, idim)

        def two_peers(step, u):
            ks = [lax.rem(grp + 1 + 2 * step + i, n_grp) for i in range(2)]
            rhs = jnp.concatenate([iq_half(k) for k in ks], axis=0)
            ws = [w2_ref[half, pl.ds(share(k), 1), :] for k in ks]
            for r in range(ZGROUP):
                raw = nt_dot(ik_all[r * t_rows:(r + 1) * t_rows, :], rhs)
                dl = dl_twice[r]
                for i in range(2):
                    coef2[u, r * t_rows:(r + 1) * t_rows, i * lanes:(i + 1) * lanes] = jnp.where(
                        raw[:, i * lanes:(i + 1) * lanes] > 0, dl * ws[i], 0.0
                    ).astype(BF16)
            grad = nn_dot(ikt_all[...], coef2[u])
            for i in range(2):
                qs_ref[half, 2 * step + i] = grad[:, i * lanes:(i + 1) * lanes]

        def send(slot):
            k = lax.rem(grp + 1 + slot, n_grp)
            pltpu.make_async_remote_copy(
                qs_ref.at[half, slot], q_recv.at[half, slot], qr_ssem.at[half], qr_rsem.at[half],
                device_id=(share(k), pb), device_id_type=MESH,
            ).start()

        @pl.loop(0, n_grp // 4)
        def _(step):
            two_peers(2 * step, 0)
            send(4 * step)
            send(4 * step + 1)
            two_peers(2 * step + 1, 1)
            send(4 * step + 2)

            @pl.when(step < n_grp // 4 - 1)
            def _():
                send(4 * step + 3)
                if between is not None:
                    between()

    query_half(0, None)

    @pl.loop(KSPLIT, pairs // 4)
    def _(step):
        key_step(step)

    @pl.loop(1, n_ctx)
    def _(r):
        peer = ctx_peer(r)
        pltpu.make_async_remote_copy(
            t_send.at[peer], t_recv.at[r - 1], send_sem.at[5], recv_sem.at[5],
            device_id=(peer, pb), device_id_type=MESH,
        ).start()

    core = lax.rem(pb, 2)
    mate = pb + 1 - 2 * core
    across = lax.rem(pb + 2, n_pb)
    own_rows = pl.ds(core * half_rows, half_rows)
    pltpu.make_async_remote_copy(
        kp_ref.at[pl.ds((1 - core) * half_rows, half_rows)], kc_ref, kp_ssem.at[0], kp_rsem.at[0],
        device_id=(ctx, mate), device_id_type=MESH,
    ).start()


    def hand_round():
        wait_bytes(t_recv.at[pl.ds(0, n_ctx - 1)], recv_sem.at[5])
        w_total = jnp.sum(t_recv[0:n_ctx - 1], axis=0) + t_send[ctx]
        w_send[...] = w_total
        kl_ref[...] = w_total[2:3, :]

        @pl.loop(1, n_ctx)
        def _(r):
            pltpu.make_async_remote_copy(
                w_send, w_recv.at[ctx], send_sem.at[9], recv_sem.at[9],
                device_id=(ctx_peer(r), pb), device_id_type=MESH,
            ).start()

    def key_across():
        wait_bytes(kc_ref, kp_rsem.at[0])
        kh_ref[0] = kp_ref[own_rows, :] + kc_ref[...]
        pltpu.make_async_remote_copy(
            kh_ref.at[0], kh_ref.at[1], kp_ssem.at[1], kp_rsem.at[1],
            device_id=(ctx, across), device_id_type=MESH,
        ).start()
        hand_round()

    query_half(1, key_across)

    wait_bytes(kh_ref.at[1], kp_rsem.at[1])
    ko_ref[core] = kh_ref[0] + kh_ref[1]
    pltpu.make_async_remote_copy(
        ko_ref.at[core], ko_ref.at[core], kp_ssem.at[2], kp_rsem.at[2],
        device_id=(ctx, mate), device_id_type=MESH,
    ).start()

    wait_bytes(w_recv.at[pl.ds(0, n_ctx - 1)], recv_sem.at[9])
    w_recv[ctx] = w_send[...]
    for i in range(n_ctx):
        wg_ref[2 * i:2 * i + 2, :] = w_recv[i, 0:2, :]

    for half in range(2):
        wait_bytes(q_recv.at[half], qr_rsem.at[half])
        total = qs_ref[half, n_grp - 1]
        for k in range(n_grp - 1):
            total = total + q_recv[half, k]
        total = total.T
        for h in range(2):
            qg_ref[h, half * half_lanes:(half + 1) * half_lanes, :] = total[h * half_lanes:(h + 1) * half_lanes]

    wait_bytes(ko_ref.at[0], kp_rsem.at[2])
    for i in range(2):
        key_ref[i * half_rows:(i + 1) * half_rows, :] = ko_ref[i]

    wait_bytes(kc_ref, kp_ssem.at[0])
    wait_bytes(kc_ref, kp_ssem.at[1])
    wait_bytes(kc_ref, kp_ssem.at[2])
    wait_bytes(key_gather, send_sem.at[0])
    wait_bytes(ist_recv.at[pl.ds(0, n_ctx - 1)], send_sem.at[1])
    for part in range(2):
        wait_bytes(st_recv.at[part, pl.ds(0, n_ctx - 1)], st_ssem.at[part])
        wait_bytes(lse_recv.at[part, pl.ds(0, n_ctx - 1)], lse_ssem.at[part])
        wait_bytes(dl_gather.at[part], zd_ssem.at[part])
        wait_bytes(q_recv.at[part], qr_ssem.at[part])
    wait_bytes(t_recv.at[pl.ds(0, n_ctx - 1)], send_sem.at[5])
    wait_bytes(w_recv.at[pl.ds(0, n_ctx - 1)], send_sem.at[9])


def hand_on(*refs):
    for source, target in zip(refs[:4], refs[4:]):
        target[...] = source[...]


def local(queries, key_cache, index_queries, index_keys, head_weights, positions, valid_lengths):
    n_ctx, n_pb = lax.axis_size("ctx"), lax.axis_size("pb")
    q_rows, lanes, lat = queries.shape
    t_rows, idim = index_keys.shape
    heads = index_queries.shape[0]
    blocks = q_rows // QBLOCK
    n_grp = n_ctx // ZGROUP
    depth = -(-(lanes + lat) // 256) * 256
    loss_scale = t_rows * n_ctx / (q_rows * n_pb)
    vmem = pltpu.VMEM
    tile = (8, lanes)
    scratch = [
        vmem((heads, q_rows, idim), BF16),
        vmem((lat, t_rows), BF16),
        vmem((2, QBLOCK, depth, lanes), BF16),
        vmem((t_rows, depth), BF16),
        vmem((t_rows, QBLOCK * lanes), F32),
        vmem((8, 2 * lanes), F32),
        vmem((blocks, t_rows, QBLOCK * lanes), BF16),
        vmem((t_rows, lanes), F32),
        vmem((t_rows, lanes), F32),
        vmem((q_rows, lanes), F32),
        vmem((lanes, q_rows), F32),
        vmem((lanes, q_rows), F32),
        vmem((TSTEP * QBLOCK * lanes, 2 * lanes), BF16),
        vmem((t_rows, 2 * lanes), F32),
        vmem((idim, ZGROUP * t_rows), BF16),
        vmem((ZGROUP * t_rows, idim), BF16),
        vmem((t_rows, 8 * lanes), BF16),
        vmem((2, ZGROUP * t_rows, 2 * lanes), BF16),
        vmem((2, heads // 2, lanes), F32),
        vmem((heads // 2, t_rows, 2 * lanes), F32),
        vmem((t_rows, idim), F32),
        vmem((ZGROUP - 1, t_rows, idim), F32),
        vmem((2, t_rows // 2, lanes), F32),
        vmem((2, ZGROUP - 1, t_rows // 2, lanes), F32),
        vmem((ZGROUP, t_rows, lanes), F32),
        vmem(tile, F32),
        vmem((n_ctx, *tile), F32),
        vmem((2, n_ctx, *tile), F32),
        vmem((2, n_ctx, *tile), F32),
        vmem((2, *tile), F32),
        vmem((2, n_ctx, *tile), F32),
        vmem((t_rows, idim), F32),
        vmem((t_rows // 2, idim), F32),
        vmem((2, t_rows // 2, idim), F32),
        vmem((2, t_rows // 2, idim), F32),
        vmem((n_ctx, *tile), F32),
        vmem((n_ctx, *tile), F32),
        vmem(tile, F32),
        vmem((n_ctx, *tile), F32),
        vmem((2, n_grp, idim, lanes), F32),
        vmem((2, n_grp - 1, idim, lanes), F32),
        pltpu.SemaphoreType.DMA,
        pltpu.SemaphoreType.DMA,
        pltpu.SemaphoreType.DMA((2,)),
        pltpu.SemaphoreType.DMA((10,)),
        pltpu.SemaphoreType.DMA((10,)),
        pltpu.SemaphoreType.DMA((ZGROUP - 1,)),
        pltpu.SemaphoreType.DMA((2, ZGROUP - 1)),
    ] + [pltpu.SemaphoreType.DMA((2,))] * 7 + [pltpu.SemaphoreType.DMA((3,))] * 2
    on_chip = pl.BlockSpec(memory_space=pltpu.VMEM)
    in_hbm = pl.BlockSpec(memory_space=pl.ANY)
    results = pl.pallas_call(
        functools.partial(kernel, n_ctx, n_pb, loss_scale),
        out_shape=(
            jax.ShapeDtypeStruct((1, q_rows), F32),
            jax.ShapeDtypeStruct((t_rows, idim), F32),
            jax.ShapeDtypeStruct((heads // n_ctx, q_rows, idim), F32),
            jax.ShapeDtypeStruct((heads, q_rows), F32),
        ),
        in_specs=[in_hbm, in_hbm, in_hbm] + [on_chip] * 4,
        out_specs=(on_chip,) * 4,
        scratch_shapes=scratch,
        compiler_params=pltpu.CompilerParams(
            collective_id=0, has_side_effects=True, vmem_limit_bytes=60 * 1024 * 1024
        ),
    )(
        queries.transpose(0, 2, 1),
        key_cache.T,
        index_queries,
        index_keys,
        head_weights.T,
        positions.reshape(1, q_rows),
        valid_lengths.reshape(1, q_rows),
    )
    kl, key_grad, query_grad, weight_grad = pl.pallas_call(
        hand_on,
        out_shape=tuple(jax.ShapeDtypeStruct(x.shape, x.dtype) for x in results),
        in_specs=[on_chip] * 4,
        out_specs=(on_chip,) * 4,
    )(*results)
    return kl.reshape(q_rows), key_grad, query_grad, weight_grad.T


def solution(mesh):
    in_specs = (
        P("pb", None, None),
        P("ctx", None),
        P(None, "pb", None),
        P("ctx", None),
        P("pb", None),
        P("pb"),
        P("pb"),
    )
    out_specs = (P("pb"), P("ctx", None), P("ctx", "pb", None), P("pb", None))
    return jax.shard_map(local, mesh=mesh, in_specs=in_specs, out_specs=out_specs, check_vma=False)
```

```python
import functools
import math

import jax
import jax.numpy as jnp
from jax import lax
from jax.experimental import pallas as pl
from jax.experimental.pallas import tpu as pltpu
from jax.sharding import PartitionSpec as P

NEG = -1e30
LOG2E = math.log2(math.e)
MESH = pl.DeviceIdType.MESH
F32 = jnp.float32
BF16 = jnp.bfloat16
ZGROUP = 4
QBLOCK = 8
KSPLIT = 5
TSTEP = 8
OWNED = 2


def nt_dot(lhs, rhs):
    return lax.dot_general(lhs, rhs, (((1,), (1,)), ((), ())), preferred_element_type=F32)


def nn_dot(lhs, rhs):
    return jnp.dot(lhs, rhs, preferred_element_type=F32)


def wait_bytes(ref, sem):
    pltpu.make_async_copy(ref, ref, sem).wait()


def kernel(
    n_ctx, n_pb, loss_scale,
    q_hbm, kt_hbm, iq_hbm, ik_ref, wt_ref, pos_ref, len_ref,
    kl_ref, key_ref, qg_ref, wg_ref,
    iq_ref, kt_ref, qb, ke, s_ref, peak_ref, p_ref, logit_ref, dl_ref, fac_ref, fact_hi, fact_lo, f_ref, tacc,
    ikt_all, ik_all, coef, coef2, w2_ref, relu_ref,
    key_send, key_gather, dl_send, dl_gather, dl_twice,
    ist_send, ist_recv, st_send, st_recv, lse_send, lse_recv,
    kp_ref, kc_ref, kh_ref, ko_ref, t_send, t_recv, w_send, w_recv, qs_ref, q_recv,
    iq_sem, kt_sem, q_sem, send_sem, recv_sem, zk_sem, zd_sem,
    st_ssem, st_rsem, lse_ssem, lse_rsem, zd_ssem, qr_ssem, qr_rsem, kp_ssem, kp_rsem,
):
    ctx = lax.axis_index("ctx")
    pb = lax.axis_index("pb")
    z = lax.rem(ctx, ZGROUP)
    grp = ctx // ZGROUP
    n_grp = n_ctx // ZGROUP
    heads = iq_ref.shape[0]
    pairs = heads // 2
    queries, lat, lanes = q_hbm.shape
    half_lanes = lanes // 2
    half_rows = ik_ref.shape[0] // 2
    t_rows = ik_ref.shape[0]
    idim = ik_ref.shape[1]
    blocks = queries // QBLOCK
    split = blocks // 2
    iscale = idim ** -0.5
    mscale = 192 ** -0.5 * LOG2E

    def ctx_peer(r):
        return lax.rem(ctx + r, n_ctx)

    def pb_peer(r):
        return lax.rem(pb + r, n_pb)

    def z_peer(r):
        return grp * ZGROUP + lax.rem(z + r, ZGROUP)

    def q_copy(block, slot):
        return pltpu.make_async_copy(
            q_hbm.at[pl.ds(block * QBLOCK, QBLOCK)],
            qb.at[slot, :, pl.ds(0, lat), :],
            q_sem.at[slot],
        )

    kt_copy = pltpu.make_async_copy(kt_hbm, kt_ref, kt_sem)
    kt_copy.start()
    q_copy(0, 0).start()
    q_copy(1, 1).start()
    iq_copy = pltpu.make_async_copy(iq_hbm, iq_ref, iq_sem)
    iq_copy.start()

    barrier = pltpu.get_barrier_semaphore()

    @pl.loop(1, n_ctx)
    def _(r):
        pl.semaphore_signal(barrier, inc=1, device_id=(ctx_peer(r), pb), device_id_type=MESH)

    @pl.loop(1, n_pb)
    def _(r):
        pl.semaphore_signal(barrier, inc=1, device_id=(ctx, pb_peer(r)), device_id_type=MESH)

    t_index = ctx * t_rows + lax.broadcasted_iota(jnp.int32, (t_rows, lanes), 0)
    pos = pos_ref[...]
    visible = (t_index <= pos) & (t_index > pos - len_ref[...])
    bias = jnp.where(visible, 0.0, NEG)
    hidden = ke.shape[1] - lanes
    kt_copy.wait()
    ke[:, 0:lat] = kt_ref[...].astype(F32).T.astype(BF16)
    ke[:, lat:hidden] = jnp.zeros((t_rows, hidden - lat), BF16)
    ke[:, hidden:] = bias.astype(BF16)
    for slot in range(2):
        for i in range(QBLOCK):
            qb[slot, i, lat:hidden, :] = jnp.zeros((hidden - lat, lanes), BF16)

    w_even = wt_ref[pl.ds(0, pairs, stride=2), :] * iscale
    w_odd = wt_ref[pl.ds(1, pairs, stride=2), :] * iscale
    first_lanes = lax.broadcasted_iota(jnp.int32, (pairs, lanes), 1) < half_lanes
    w2_ref[0] = jnp.where(first_lanes, w_even, pltpu.roll(w_odd, half_lanes, 1))
    w2_ref[1] = jnp.where(first_lanes, pltpu.roll(w_even, half_lanes, 1), w_odd)

    ik = ik_ref[...]
    key_send[...] = ik.astype(F32)

    pl.semaphore_wait(barrier, n_ctx - 1 + n_pb - 1)

    for r in range(1, ZGROUP):
        pltpu.make_async_remote_copy(
            key_send, key_gather.at[r - 1], send_sem.at[0], zk_sem.at[r - 1],
            device_id=(z_peer(r), pb), device_id_type=MESH,
        ).start()

    st_send[...] = jnp.zeros_like(st_send)

    def exponentials(block):
        part = block // split
        for u in range(QBLOCK // 2):
            peak = peak_ref[u:u + 1, :]
            expo = jnp.exp2(s_ref[:, 2 * u * lanes:(2 * u + 2) * lanes] * mscale - peak)
            total = jnp.sum(expo, axis=0, keepdims=True)
            p_ref[block, :, 2 * u * lanes:(2 * u + 2) * lanes] = expo.astype(BF16)
            for h in range(2):
                i = 2 * u + h
                owner = QBLOCK // OWNED * lax.rem(block, split) + i // OWNED
                st_send[part, owner, pl.ds(i % OWNED, 1), :] = peak[:, h * lanes:(h + 1) * lanes]
                st_send[part, owner, pl.ds(4 + i % OWNED, 1), :] = total[:, h * lanes:(h + 1) * lanes]

    def scores(block):
        slot = lax.rem(block, 2)
        q_copy(block, slot).wait()
        row = lax.broadcasted_iota(jnp.int32, (lanes, lanes), 0)
        for i in range(QBLOCK):
            qb[slot, i, hidden:, :] = jnp.where(row == block * QBLOCK + i, 1.0, 0.0).astype(BF16)
        exponentials(lax.max(block - 1, 0))
        rhs = jnp.concatenate([qb[slot, i] for i in range(QBLOCK)], axis=1)
        s = nn_dot(ke[...], rhs)
        s_ref[...] = s
        peak = jnp.max(s, axis=0, keepdims=True) * mscale
        for u in range(QBLOCK // 2):
            peak_ref[u:u + 1, :] = peak[:, 2 * u * lanes:(2 * u + 2) * lanes]

        @pl.when(block + 2 < blocks)
        def _():
            q_copy(block + 2, slot).start()

    def send_stats(part):
        @pl.loop(1, n_ctx)
        def _(r):
            peer = ctx_peer(r)
            pltpu.make_async_remote_copy(
                st_send.at[part, peer], st_recv.at[part, r - 1], st_ssem.at[part], st_rsem.at[part],
                device_id=(peer, pb), device_id_type=MESH,
            ).start()

    def combine(part):
        wait_bytes(st_recv.at[part, pl.ds(0, n_ctx - 1)], st_rsem.at[part])
        st_recv[part, n_ctx - 1] = st_send[part, ctx]
        got = st_recv[part]
        peaks, sums = got[:, 0:4, :], got[:, 4:8, :]
        top = jnp.max(peaks, axis=0)
        total = jnp.sum(sums * jnp.exp2(peaks - top[None]), axis=0)
        lse_send[part] = jnp.zeros((8, lanes), F32)
        lse_send[part, 0:4, :] = top + jnp.log(jnp.maximum(total, 1e-30)) * LOG2E

        @pl.loop(1, n_ctx)
        def _(r):
            pltpu.make_async_remote_copy(
                lse_send.at[part], lse_recv.at[part, ctx], lse_ssem.at[part], lse_rsem.at[part],
                device_id=(ctx_peer(r), pb), device_id_type=MESH,
            ).start()

    def factors(part):
        wait_bytes(lse_recv.at[part, pl.ds(0, n_ctx - 1)], lse_rsem.at[part])
        lse_recv[part, ctx] = lse_send[part]
        for i in range(n_ctx):
            row = part * OWNED * n_ctx + OWNED * i
            fac_ref[row:row + OWNED, :] = jnp.exp2(
                st_send[part, i, 0:OWNED, :] - lse_recv[part, i, 0:OWNED, :]
            )
        fact = fac_ref[...].T * (1.0 / lanes)
        hi = fact.astype(BF16)
        fact_hi[...] = hi.astype(F32)
        fact_lo[...] = fact - hi.astype(F32)

    @pl.loop(0, split + 1)
    def _(block):
        scores(block)

    send_stats(0)

    @pl.loop(split + 1, blocks)
    def _(block):
        scores(block)

    exponentials(blocks - 1)
    send_stats(1)
    combine(0)

    iq_copy.wait()
    logit_ref[...] = jnp.zeros_like(logit_ref)

    @pl.loop(0, pairs // 4)
    def _(step):
        total = logit_ref[...]
        for u in range(4):
            jp = step * 4 + u
            raw = nt_dot(ik, iq_ref[pl.ds(2 * jp, 2)].reshape(2 * lanes, idim))
            w = wt_ref[pl.ds(2 * jp, 2), :]
            active = jnp.maximum(raw, 0.0)
            relu_ref[jp] = active
            total = total + active[:, :lanes] * w[0:1]
            total = total + active[:, lanes:] * w[1:2]
        logit_ref[...] = total

    logits = logit_ref[...] * (iscale * LOG2E) + bias
    logit_ref[...] = logits
    i_peak = jnp.max(logits, axis=0, keepdims=True)
    i_sum = jnp.sum(jnp.exp2(logits - i_peak), axis=0, keepdims=True)
    ist_send[...] = jnp.zeros_like(ist_send)
    ist_send[0:1, :] = i_peak
    ist_send[1:2, :] = i_sum

    @pl.loop(1, n_ctx)
    def _(r):
        pltpu.make_async_remote_copy(
            ist_send, ist_recv.at[r - 1], send_sem.at[1], recv_sem.at[1],
            device_id=(ctx_peer(r), pb), device_id_type=MESH,
        ).start()

    combine(1)

    ik_all[0:t_rows, :] = ik
    ikt_all[:, 0:t_rows] = key_send[...].T.astype(BF16)
    for r in range(1, ZGROUP):
        wait_bytes(key_gather.at[r - 1], zk_sem.at[r - 1])
        got = key_gather[r - 1]
        ik_all[r * t_rows:(r + 1) * t_rows, :] = got.astype(BF16)
        ikt_all[:, r * t_rows:(r + 1) * t_rows] = got.T.astype(BF16)

    tacc[...] = jnp.zeros_like(tacc)

    def add_target(step):
        lane = lax.broadcasted_iota(jnp.int32, (lanes, lanes), 1)
        for i in range(TSTEP * QBLOCK):
            here = lane == step * (TSTEP * QBLOCK) + i
            f_ref[i * lanes:(i + 1) * lanes, 0:lanes] = jnp.where(here, fact_hi[...], 0.0).astype(BF16)
            f_ref[i * lanes:(i + 1) * lanes, lanes:] = jnp.where(here, fact_lo[...], 0.0).astype(BF16)
        wide = jnp.concatenate([p_ref[TSTEP * step + u] for u in range(TSTEP)], axis=1)
        tacc[...] += nn_dot(wide, f_ref[...])

    lower = lax.broadcasted_iota(jnp.int32, (half_rows, lanes), 1) < half_lanes

    def swap(x):
        return pltpu.roll(x, half_lanes, 1)

    def send_dlogit(half, dl):
        top, bottom = dl[:half_rows], dl[half_rows:]
        if half == 0:
            dl_send[half] = jnp.where(lower, top, swap(bottom))
        else:
            dl_send[half] = jnp.where(lower, swap(top), bottom)
        for r in range(1, ZGROUP):
            pltpu.make_async_remote_copy(
                dl_send.at[half], dl_gather.at[half, r - 1], zd_ssem.at[half], zd_sem.at[half, r - 1],
                device_id=(z_peer(r), pb), device_id_type=MESH,
            ).start()

    factors(0)

    @pl.loop(0, split // TSTEP)
    def _(step):
        add_target(step)

    wait_bytes(ist_recv.at[pl.ds(0, n_ctx - 1)], recv_sem.at[1])
    ist_recv[n_ctx - 1] = ist_send[...]
    got = ist_recv[...]
    peaks, sums = got[:, 0:1, :], got[:, 1:2, :]
    top = jnp.max(peaks, axis=0)
    i_lse = top + jnp.log(jnp.sum(sums * jnp.exp2(peaks - top[None]), axis=0)) * LOG2E

    index_prob = jnp.exp2(logit_ref[...] - i_lse)
    send_dlogit(0, loss_scale * (index_prob - (tacc[:, 0:lanes] + tacc[:, lanes:])))

    factors(1)

    @pl.loop(split // TSTEP, blocks // TSTEP)
    def _(step):
        add_target(step)

    target = tacc[:, 0:lanes] + tacc[:, lanes:]
    log_index = logit_ref[...] - i_lse
    index_prob = jnp.exp2(log_index)
    dl_ref[...] = loss_scale * (index_prob - target)
    send_dlogit(1, dl_ref[...])
    positive = target > 0
    log_target = jnp.log(jnp.where(positive, target, 1.0))
    kl = jnp.sum(
        jnp.where(positive, target * (log_target - log_index * math.log(2.0)), 0.0), axis=0, keepdims=True
    )

    kp_ref[...] = jnp.zeros_like(kp_ref)

    def key_step(step):
        dl = dl_ref[...]
        for u in range(4):
            jp = step * 4 + u
            w = wt_ref[pl.ds(2 * jp, 2), :] * iscale
            for h in range(2):
                part = relu_ref[jp, :, h * lanes:(h + 1) * lanes]
                t_send[jp, pl.ds(h, 1), :] = jnp.sum(dl * part, axis=0, keepdims=True) * iscale
                coef[:, (2 * u + h) * lanes:(2 * u + h + 1) * lanes] = jnp.where(
                    part > 0, dl * w[h:h + 1], 0.0
                ).astype(BF16)
            t_send[jp, pl.ds(2, 1), :] = kl
            t_send[jp, pl.ds(3, 5), :] = jnp.zeros((5, lanes), F32)
        kp_ref[...] += nn_dot(coef[...], iq_ref[pl.ds(8 * step, 8)].reshape(8 * lanes, idim))

    @pl.loop(0, KSPLIT)
    def _(step):
        key_step(step)

    def query_half(half, between):
        for r in range(ZGROUP):
            if r:
                wait_bytes(dl_gather.at[half, r - 1], zd_sem.at[half, r - 1])
            packed = dl_gather[half, r - 1] if r else dl_send[half]
            other = swap(packed)
            dl_twice[r, 0:half_rows, :] = jnp.where(lower, packed, other)
            dl_twice[r, half_rows:, :] = jnp.where(lower, other, packed)

        def share(k):
            return k * ZGROUP + z

        def iq_half(k):
            part = iq_ref[pl.ds(2 * share(k), 2), half * half_lanes:(half + 1) * half_lanes, :]
            return part.reshape(lanes, idim)

        def two_peers(step, u):
            ks = [lax.rem(grp + 1 + 2 * step + i, n_grp) for i in range(2)]
            rhs = jnp.concatenate([iq_half(k) for k in ks], axis=0)
            ws = [w2_ref[half, pl.ds(share(k), 1), :] for k in ks]
            for r in range(ZGROUP):
                raw = nt_dot(ik_all[r * t_rows:(r + 1) * t_rows, :], rhs)
                dl = dl_twice[r]
                for i in range(2):
                    coef2[u, r * t_rows:(r + 1) * t_rows, i * lanes:(i + 1) * lanes] = jnp.where(
                        raw[:, i * lanes:(i + 1) * lanes] > 0, dl * ws[i], 0.0
                    ).astype(BF16)
            grad = nn_dot(ikt_all[...], coef2[u])
            for i in range(2):
                qs_ref[half, 2 * step + i] = grad[:, i * lanes:(i + 1) * lanes]

        def send(slot):
            k = lax.rem(grp + 1 + slot, n_grp)
            pltpu.make_async_remote_copy(
                qs_ref.at[half, slot], q_recv.at[half, slot], qr_ssem.at[half], qr_rsem.at[half],
                device_id=(share(k), pb), device_id_type=MESH,
            ).start()

        @pl.loop(0, n_grp // 4)
        def _(step):
            two_peers(2 * step, 0)
            send(4 * step)
            send(4 * step + 1)
            two_peers(2 * step + 1, 1)
            send(4 * step + 2)

            @pl.when(step < n_grp // 4 - 1)
            def _():
                send(4 * step + 3)
                if between is not None:
                    between()

    query_half(0, None)

    @pl.loop(KSPLIT, pairs // 4)
    def _(step):
        key_step(step)

    @pl.loop(1, n_ctx)
    def _(r):
        peer = ctx_peer(r)
        pltpu.make_async_remote_copy(
            t_send.at[peer], t_recv.at[r - 1], send_sem.at[5], recv_sem.at[5],
            device_id=(peer, pb), device_id_type=MESH,
        ).start()

    core = lax.rem(pb, 2)
    mate = pb + 1 - 2 * core
    across = lax.rem(pb + 2, n_pb)
    own_rows = pl.ds(core * half_rows, half_rows)
    pltpu.make_async_remote_copy(
        kp_ref.at[pl.ds((1 - core) * half_rows, half_rows)], kc_ref, kp_ssem.at[0], kp_rsem.at[0],
        device_id=(ctx, mate), device_id_type=MESH,
    ).start()


    def hand_round():
        wait_bytes(t_recv.at[pl.ds(0, n_ctx - 1)], recv_sem.at[5])
        w_total = jnp.sum(t_recv[0:n_ctx - 1], axis=0) + t_send[ctx]
        w_send[...] = w_total
        kl_ref[...] = w_total[2:3, :]

        @pl.loop(1, n_ctx)
        def _(r):
            pltpu.make_async_remote_copy(
                w_send, w_recv.at[ctx], send_sem.at[9], recv_sem.at[9],
                device_id=(ctx_peer(r), pb), device_id_type=MESH,
            ).start()

    def key_across():
        wait_bytes(kc_ref, kp_rsem.at[0])
        kh_ref[0] = kp_ref[own_rows, :] + kc_ref[...]
        pltpu.make_async_remote_copy(
            kh_ref.at[0], kh_ref.at[1], kp_ssem.at[1], kp_rsem.at[1],
            device_id=(ctx, across), device_id_type=MESH,
        ).start()
        hand_round()

    query_half(1, key_across)

    wait_bytes(kh_ref.at[1], kp_rsem.at[1])
    ko_ref[core] = kh_ref[0] + kh_ref[1]
    pltpu.make_async_remote_copy(
        ko_ref.at[core], ko_ref.at[core], kp_ssem.at[2], kp_rsem.at[2],
        device_id=(ctx, mate), device_id_type=MESH,
    ).start()

    wait_bytes(w_recv.at[pl.ds(0, n_ctx - 1)], recv_sem.at[9])
    w_recv[ctx] = w_send[...]
    for i in range(n_ctx):
        wg_ref[2 * i:2 * i + 2, :] = w_recv[i, 0:2, :]

    for half in range(2):
        wait_bytes(q_recv.at[half], qr_rsem.at[half])
        total = qs_ref[half, n_grp - 1]
        for k in range(n_grp - 1):
            total = total + q_recv[half, k]
        total = total.T
        for h in range(2):
            qg_ref[h, half * half_lanes:(half + 1) * half_lanes, :] = total[h * half_lanes:(h + 1) * half_lanes]

    wait_bytes(ko_ref.at[0], kp_rsem.at[2])
    for i in range(2):
        key_ref[i * half_rows:(i + 1) * half_rows, :] = ko_ref[i]

    wait_bytes(kc_ref, kp_ssem.at[0])
    wait_bytes(kc_ref, kp_ssem.at[1])
    wait_bytes(kc_ref, kp_ssem.at[2])
    wait_bytes(key_gather, send_sem.at[0])
    wait_bytes(ist_recv.at[pl.ds(0, n_ctx - 1)], send_sem.at[1])
    for part in range(2):
        wait_bytes(st_recv.at[part, pl.ds(0, n_ctx - 1)], st_ssem.at[part])
        wait_bytes(lse_recv.at[part, pl.ds(0, n_ctx - 1)], lse_ssem.at[part])
        wait_bytes(dl_gather.at[part], zd_ssem.at[part])
        wait_bytes(q_recv.at[part], qr_ssem.at[part])
    wait_bytes(t_recv.at[pl.ds(0, n_ctx - 1)], send_sem.at[5])
    wait_bytes(w_recv.at[pl.ds(0, n_ctx - 1)], send_sem.at[9])


def hand_on(*refs):
    for source, target in zip(refs[:4], refs[4:]):
        target[...] = source[...]


def local(queries, key_cache, index_queries, index_keys, head_weights, positions, valid_lengths):
    n_ctx, n_pb = lax.axis_size("ctx"), lax.axis_size("pb")
    q_rows, lanes, lat = queries.shape
    t_rows, idim = index_keys.shape
    heads = index_queries.shape[0]
    blocks = q_rows // QBLOCK
    n_grp = n_ctx // ZGROUP
    depth = -(-(lanes + lat) // 256) * 256
    loss_scale = t_rows * n_ctx / (q_rows * n_pb)
    vmem = pltpu.VMEM
    tile = (8, lanes)
    scratch = [
        vmem((heads, q_rows, idim), BF16),
        vmem((lat, t_rows), BF16),
        vmem((2, QBLOCK, depth, lanes), BF16),
        vmem((t_rows, depth), BF16),
        vmem((t_rows, QBLOCK * lanes), F32),
        vmem((8, 2 * lanes), F32),
        vmem((blocks, t_rows, QBLOCK * lanes), BF16),
        vmem((t_rows, lanes), F32),
        vmem((t_rows, lanes), F32),
        vmem((q_rows, lanes), F32),
        vmem((lanes, q_rows), F32),
        vmem((lanes, q_rows), F32),
        vmem((TSTEP * QBLOCK * lanes, 2 * lanes), BF16),
        vmem((t_rows, 2 * lanes), F32),
        vmem((idim, ZGROUP * t_rows), BF16),
        vmem((ZGROUP * t_rows, idim), BF16),
        vmem((t_rows, 8 * lanes), BF16),
        vmem((2, ZGROUP * t_rows, 2 * lanes), BF16),
        vmem((2, heads // 2, lanes), F32),
        vmem((heads // 2, t_rows, 2 * lanes), F32),
        vmem((t_rows, idim), F32),
        vmem((ZGROUP - 1, t_rows, idim), F32),
        vmem((2, t_rows // 2, lanes), F32),
        vmem((2, ZGROUP - 1, t_rows // 2, lanes), F32),
        vmem((ZGROUP, t_rows, lanes), F32),
        vmem(tile, F32),
        vmem((n_ctx, *tile), F32),
        vmem((2, n_ctx, *tile), F32),
        vmem((2, n_ctx, *tile), F32),
        vmem((2, *tile), F32),
        vmem((2, n_ctx, *tile), F32),
        vmem((t_rows, idim), F32),
        vmem((t_rows // 2, idim), F32),
        vmem((2, t_rows // 2, idim), F32),
        vmem((2, t_rows // 2, idim), F32),
        vmem((n_ctx, *tile), F32),
        vmem((n_ctx, *tile), F32),
        vmem(tile, F32),
        vmem((n_ctx, *tile), F32),
        vmem((2, n_grp, idim, lanes), F32),
        vmem((2, n_grp - 1, idim, lanes), F32),
        pltpu.SemaphoreType.DMA,
        pltpu.SemaphoreType.DMA,
        pltpu.SemaphoreType.DMA((2,)),
        pltpu.SemaphoreType.DMA((10,)),
        pltpu.SemaphoreType.DMA((10,)),
        pltpu.SemaphoreType.DMA((ZGROUP - 1,)),
        pltpu.SemaphoreType.DMA((2, ZGROUP - 1)),
    ] + [pltpu.SemaphoreType.DMA((2,))] * 7 + [pltpu.SemaphoreType.DMA((3,))] * 2
    on_chip = pl.BlockSpec(memory_space=pltpu.VMEM)
    in_hbm = pl.BlockSpec(memory_space=pl.ANY)
    results = pl.pallas_call(
        functools.partial(kernel, n_ctx, n_pb, loss_scale),
        out_shape=(
            jax.ShapeDtypeStruct((1, q_rows), F32),
            jax.ShapeDtypeStruct((t_rows, idim), F32),
            jax.ShapeDtypeStruct((heads // n_ctx, q_rows, idim), F32),
            jax.ShapeDtypeStruct((heads, q_rows), F32),
        ),
        in_specs=[in_hbm, in_hbm, in_hbm] + [on_chip] * 4,
        out_specs=(on_chip,) * 4,
        scratch_shapes=scratch,
        compiler_params=pltpu.CompilerParams(
            collective_id=0, has_side_effects=True, vmem_limit_bytes=60 * 1024 * 1024
        ),
    )(
        queries.transpose(0, 2, 1),
        key_cache.T,
        index_queries,
        index_keys,
        head_weights.T,
        positions.reshape(1, q_rows),
        valid_lengths.reshape(1, q_rows),
    )
    kl, key_grad, query_grad, weight_grad = pl.pallas_call(
        hand_on,
        out_shape=tuple(jax.ShapeDtypeStruct(x.shape, x.dtype) for x in results),
        in_specs=[on_chip] * 4,
        out_specs=(on_chip,) * 4,
    )(*results)
    return kl.reshape(q_rows), key_grad, query_grad, weight_grad.T


def solution(mesh):
    in_specs = (
        P("pb", None, None),
        P("ctx", None),
        P(None, "pb", None),
        P("ctx", None),
        P("pb", None),
        P("pb"),
        P("pb"),
    )
    out_specs = (P("pb"), P("ctx", None), P("ctx", "pb", None), P("pb", None))
    return jax.shard_map(local, mesh=mesh, in_specs=in_specs, out_specs=out_specs, check_vma=False)
```
